256 devices in a mesh: tm: 128 (over y, z, x), space: 2 (over core).
Axes of the slice: x: 4, y: 4, z: 8, core: 2. Of those that a mesh axis runs over, the one named last changes fastest.
Arguments:
- cpoints: float32 [1024, 32, 512], P('tm', 'space'), may hold values from -7 to 7
- initial: float32 [32, 512], P('space'), may hold values from -6 to 6
- diffusion: float32 [32, 512], P('space'), may hold values from 0.0005 to 0.0025
- velocity_x: float32 [32, 512], P('space'), may hold values from -0.0025 to 0.0025
- velocity_y: float32 [32, 512], P('space'), may hold values from -0.0025 to 0.0025
- source: float32 [32, 512], P('space'), may hold values from -0.018 to 0.018
Outputs:
- updated: float32 [1024, 32, 512], P('tm', 'space')
The draws below stay inside these ranges and needn't reach their ends.
All inputs are finite; a program needn't handle non-finite values.
Results may differ from the reference program's by a relative error of at most 0.000032.
Values sent between devices are 32-bit elements; how exact they have to be, the bound alone decides.
A program may use at most 64 MiB of HBM per device.

```python
import math
import jax
import jax.numpy as jnp
from jax import lax

M = 8
W = 512
NY = 32
NC = 1024
N_TM = 128


def draw_cpoints(key, part):
    key = jax.random.fold_in(key, 7)
    keys = jax.random.split(key, 5)
    rows = jnp.arange(NY, dtype=jnp.float32)
    cols = jnp.arange(W, dtype=jnp.float32)
    period = 16 * M
    spans = (NC + period - 1) // period
    phases = jax.random.uniform(keys[0], (5,), dtype=jnp.float32, minval=-jnp.pi, maxval=jnp.pi)
    weights = jax.random.uniform(keys[1], (spans, 5), dtype=jnp.float32, minval=0.2, maxval=0.6)
    parity = jnp.arange(spans, dtype=jnp.int32) % 2
    signs = jnp.where(parity == 0, 1.0, -1.0).astype(jnp.float32)[:, None]
    rough = jax.random.uniform(keys[3], (NC, NY, W), dtype=jnp.float32, minval=0.5, maxval=2.5)
    amplitudes = jnp.repeat(weights * signs, period, axis=0)[:NC]
    smooth = jnp.zeros((NC, NY, W), jnp.float32)
    for order in range(5):
        row_shape = jnp.sin(jnp.pi * (order + 1.0) * (rows + 1.0) / (NY + 1.0))
        col_shape = 1.0 + 0.4 * jnp.cos(2.0 * jnp.pi * cols / W + phases[order])
        smooth = smooth + amplitudes[:, order][:, None, None] * row_shape[None, :, None] * col_shape[None, None, :]
    checker_ids = (jnp.arange(NY, dtype=jnp.int32)[:, None] + jnp.arange(W, dtype=jnp.int32)[None, :]) % 2
    checker = jnp.where(checker_ids == 0, 1.0, -1.0).astype(jnp.float32)
    point_flips = jax.random.bernoulli(keys[4], 0.5, (NC, 1, 1))
    point_signs = jnp.where(point_flips, 1.0, -1.0).astype(jnp.float32)
    return (smooth + point_signs * checker[None] * rough).astype(jnp.float32)


def level_of(rng, shape, cuts, least, high):
    level, own = 1.0, jax.random.fold_in(rng, 6)
    for dim, shards_of in cuts:
        heights = jnp.exp(jax.random.uniform(jax.random.fold_in(own, dim), (shards_of,), jnp.float32, least / len(cuts), high / len(cuts)))
        level = level * jnp.repeat(heights, shape[dim] // shards_of).reshape([-1 if axis == dim else 1 for axis in range(len(shape))])
    return level


def normal_values(key, dims, deviation, limit, cuts=(), held_as=jnp.bfloat16):
    drawn = jax.random.normal(key, dims, jnp.float32) * deviation
    if len(cuts) > 0:
        drawn = level_of(key, dims, cuts, -0.22, 0.18) * drawn
    return jnp.clip(drawn, min=-limit, max=limit).astype(held_as)


def setup_inputs(seed: int = 0) -> dict:
    seeds = jax.random.split(jax.random.key(seed), 7)
    cpoints = draw_cpoints(jax.random.fold_in(seeds[6], 71), 0)
    initial = normal_values(seeds[1], (NY, W), 1.0, 6.0, ((0, 2),), jnp.float32)
    diffusion = jnp.clip(jnp.exp(math.log(0.0025) - 1.6094378 * jax.random.uniform(seeds[2], (NY, W), jnp.float32) ** level_of(seeds[2], (NY, W), ((0, 2),), -0.2, 0.2)), 0.0005, 0.0025)
    velocity_x = jnp.clip(jax.random.uniform(seeds[3], (NY, W), jnp.float32, -0.0025, 0.0025) * level_of(seeds[3], (NY, W), ((0, 2),), -0.4, 0.0), -0.0025, 0.0025)
    velocity_y = jnp.clip(jax.random.uniform(seeds[4], (NY, W), jnp.float32, -0.0025, 0.0025) * level_of(seeds[4], (NY, W), ((0, 2),), -0.4, 0.0), -0.0025, 0.0025)
    source = normal_values(seeds[5], (NY, W), 0.003, 0.018, ((0, 2),), jnp.float32)
    return dict(cpoints=cpoints, initial=initial, diffusion=diffusion, velocity_x=velocity_x, velocity_y=velocity_y, source=source)


def stencil(padded, diffusion, velocity_x, velocity_y, time_scale):
    centre = padded[..., 1:-1, :]
    upper_row = padded[..., :-2, :]
    lower_row = padded[..., 2:, :]
    right_col = jnp.roll(centre, -1, axis=-1)
    left_col = jnp.roll(centre, 1, axis=-1)
    spread = upper_row + lower_row + right_col + left_col - 4.0 * centre
    across = jnp.maximum(velocity_x, 0.0) * (centre - left_col) + jnp.minimum(velocity_x, 0.0) * (right_col - centre)
    downward = jnp.maximum(velocity_y, 0.0) * (centre - upper_row) + jnp.minimum(velocity_y, 0.0) * (lower_row - centre)
    return centre + time_scale * (diffusion * spread - across - downward)


def advance(snapshot, diffusion, velocity_x, velocity_y, time_scale):
    widths = [(0, 0)] * (snapshot.ndim - 2) + [(1, 1), (0, 0)]
    return stencil(jnp.pad(snapshot, widths), diffusion, velocity_x, velocity_y, time_scale)


def reference(cpoints, initial, diffusion, velocity_x, velocity_y, source):
    def relax_fine(states):
        for _ in range(M):
            states = advance(states, diffusion, velocity_x, velocity_y, 1.0) + source
        return states

    def level_step(states, time_scale):
        return advance(states, diffusion, velocity_x, velocity_y, time_scale)

    relaxed = relax_fine(jnp.concatenate([initial[None], cpoints[:-1]], axis=0))
    defect = relax_fine(jnp.concatenate([initial[None], relaxed[:-1]], axis=0)) - relaxed
    blocks = defect.reshape(N_TM, M, NY, W)
    level_c = jnp.zeros((N_TM, NY, W), jnp.float32)
    for counter in range(M):
        level_c = level_step(level_c, 8.0) + blocks[:, counter]
    empty = jnp.zeros((1, NY, W), jnp.float32)
    lagged = jnp.concatenate([empty, level_c[:-1]], axis=0)
    coarse_defect = lagged
    for _ in range(M):
        coarse_defect = level_step(coarse_defect, 8.0)

    def coarse_step(carried, addend):
        nxt = level_step(carried, 64.0) + addend
        return nxt, nxt

    _, coarse = lax.scan(coarse_step, jnp.zeros((NY, W), jnp.float32), coarse_defect)
    corrected = level_c + coarse
    walker = jnp.concatenate([empty, corrected[:-1]], axis=0)
    errors = []
    for counter in range(M - 1):
        walker = level_step(walker, 8.0) + blocks[:, counter]
        errors.append(walker)
    errors.append(corrected)
    return relaxed + jnp.stack(errors, axis=1).reshape(N_TM * M, NY, W)
```

```python
import functools

import jax
import jax.numpy as jnp
from jax import lax
from jax.experimental import pallas as pl
from jax.experimental.pallas import tpu as pltpu
from jax.sharding import PartitionSpec as P

M = 8
NX = 4
NZ = 8
C = 4
R = 4
T = (8, 128)
STATE = (C, R) + T
WIN = (R,) + T
MESH = pl.DeviceIdType.MESH
COLS = [pl.ds(128 * c, 128) for c in range(C)]


def load_state(ref, *idx):
    return [[ref[(*idx, c, r)] for r in range(R)] for c in range(C)]


def store_state(ref, v, *idx):
    for c in range(C):
        for r in range(R):
            ref[(*idx, c, r)] = v[c][r]


def load_win(ref, *idx):
    return [ref[(*idx, r)] for r in range(R)]


def store_win(ref, v, *idx):
    for r in range(R):
        ref[(*idx, r)] = v[r]


def add(a, b):
    if isinstance(a, list):
        return [add(x, y) for x, y in zip(a, b)]
    return a + b


def sub(a, b):
    if isinstance(a, list):
        return [sub(x, y) for x, y in zip(a, b)]
    return a - b


def lanes():
    return lax.broadcasted_iota(jnp.int32, T, 1)


def sublanes():
    return lax.broadcasted_iota(jnp.int32, T, 0)


def ups(column):
    return [pltpu.roll(column[R - 1], 1, 0)] + column[: R - 1]


def downs(column):
    return column[1:] + [pltpu.roll(column[0], 7, 0)]


def full_step(states, coef, source=None):
    lane = lanes()
    first, last = lane == 0, lane == 127
    out = [[[None] * R for _ in range(C)] for _ in states]
    rolled = []
    for v in states:
        to_right = [[pltpu.roll(v[c][r], 1, 1) for r in range(R)] for c in range(C)]
        to_left = [[pltpu.roll(v[c][r], 127, 1) for r in range(R)] for c in range(C)]
        rolled.append((to_right, to_left))
    for c in range(C):
        above = [ups(v[c]) for v in states]
        below = [downs(v[c]) for v in states]
        for r in range(R):
            k0, kl, kr, ku, kd = (coef[k, c, r] for k in range(5))
            plus = None if source is None else source[c, r]
            for n, v in enumerate(states):
                to_right, to_left = rolled[n]
                left = jnp.where(first, to_right[(c - 1) % C][r], to_right[c][r])
                right = jnp.where(last, to_left[(c + 1) % C][r], to_left[c][r])
                new = (k0 * v[c][r] + kl * left) + (kr * right + ku * above[n][r])
                new = new + kd * below[n][r]
                out[n][c][r] = new if plus is None else new + plus
    return out


def win_step(v, coef):
    above, below = ups(v), downs(v)
    out = []
    for r in range(R):
        left, right = pltpu.roll(v[r], 1, 1), pltpu.roll(v[r], 127, 1)
        k0, kl, kr, ku, kd = (coef[k, r] for k in range(5))
        out.append((k0 * v[r] + kl * left) + (kr * right + ku * above[r]) + kd * below[r])
    return out


def full_steps(count, states, coef, source=None):
    return lax.fori_loop(0, count, lambda _, s: full_step(s, coef, source), states)


def win_steps(count, v, coef):
    return lax.fori_loop(0, count, lambda _, s: win_step(s, coef), v)


def window_tiles(v, band):
    lane = lanes()
    low = band == 0
    shift = jnp.where(low, 32, 96)
    take = jnp.logical_or(
        jnp.logical_and(low, lane < 32), jnp.logical_and(jnp.logical_not(low), lane >= 96)
    )
    rot = [[pltpu.roll(v[c][r], shift, 1) for r in range(R)] for c in range(C)]
    out = []
    for c in range(C):
        tile = []
        for r in range(R):
            beside = jnp.where(low, rot[(c - 1) % C][r], rot[(c + 1) % C][r])
            tile.append(jnp.where(take, beside, rot[c][r]))
        out.append(tile)
    return out


def merged(own, other, band):
    lane = lanes()
    low = band == 0
    out = []
    for a, b in zip(own, other):
        w0, w1 = jnp.where(low, a, b), jnp.where(low, b, a)
        out.append(jnp.where(lane < 64, pltpu.roll(w0, 96, 1), pltpu.roll(w1, 32, 1)))
    return out


def kernel(
    n_tm, cpoints, initial, diffusion, velocity_x, velocity_y, source, out,
    cp, fld, c1, c8, c64, src, cwin, tmp, st, sp, dfc, lev, lag, w1s, w1, u1, pz,
    t2own, t2sib, t2m, t2, rown, rsib, rm, rr, fbuf, outb, send, recv, loc,
):
    p = lax.axis_index("tm")
    s = lax.axis_index("space")
    x = lax.rem(p, NX)
    g = lax.div(p, NX)
    z = lax.rem(g, NZ)
    y = lax.div(g, NZ)
    n_y = n_tm // (NX * NZ)
    plane = NX * NZ
    other = 1 - s
    row0 = pl.multiple_of(16 * s, 16)
    band = pl.ds(row0, 16)

    def dev(tm, space):
        return {"tm": tm, "space": space}

    barrier = pltpu.get_barrier_semaphore()

    def greet(tm, space):
        pl.semaphore_signal(barrier, inc=1, device_id=dev(tm, space), device_id_type=MESH)

    greet(p, other)

    @pl.when(p > 0)
    def _():
        greet(p - 1, 0)
        greet(p - 1, 1)

    for d in range(1, NX):
        greet(NX * g + lax.rem(x + d, NX), s)
    for d in range(1, NZ):
        greet(plane * y + NX * lax.rem(z + d, NZ) + x, s)
    for yy in range(n_y - 1):
        @pl.when(yy < y)
        def _():
            for xx in range(NX):
                greet(plane * yy + NX * z + xx, s)

    @pl.when(jnp.logical_and(x == 0, p > 0))
    def _():
        for d in range(1, NX + 1):
            greet(p - d, s)

    fields = (diffusion, velocity_x, velocity_y, source, initial)
    own = [pltpu.make_async_copy(f, fld.at[k, band, :], loc.at[k]) for k, f in enumerate(fields)]
    own.append(pltpu.make_async_copy(cpoints.at[pl.ds(0, 7)], cp.at[pl.ds(2, 7), band, :], loc.at[5]))
    for copy in own:
        copy.start()

    sends = 1 + (NX - 1) + (NZ - 1) + NX * (n_y - 1 - y)
    sends = sends + jnp.where(p < n_tm - 1, 2, 0)
    sends = sends + jnp.where(g < n_tm // NX - 1, 1, 0)
    pl.semaphore_wait(barrier, sends)

    def remote(src_ref, dst_ref, to, send_idx, recv_idx):
        return pltpu.make_async_remote_copy(
            src_ref=src_ref, dst_ref=dst_ref, send_sem=send.at[send_idx], recv_sem=recv.at[recv_idx],
            device_id=to, device_id_type=MESH,
        )

    sib = [
        remote(f, fld.at[k, band, :], dev(p, other), k, k) for k, f in enumerate(fields)
    ]
    sib.append(
        remote(cpoints.at[pl.ds(0, 7)], cp.at[pl.ds(2, 7), band, :], dev(p, other), 5, 5)
    )
    for copy in sib:
        copy.start()
    tail = cpoints.at[pl.ds(6, 2)]
    head = cp.at[pl.ds(0, 2), band, :]
    ahead = [remote(tail, head, dev(p + 1, ss), 6 + ss, 6 + s) for ss in range(2)]

    @pl.when(p < n_tm - 1)
    def _():
        for copy in ahead:
            copy.start()

    for copy in own[:5]:
        copy.wait()
    for copy in sib[:5]:
        copy.wait_recv()

    def rows_in(ref, k, slot):
        for c in range(C):
            for t in range(4):
                tmp[slot, c, pl.ds(8 * t, 8), :] = ref[k, pl.ds(8 * t, 8), COLS[c]]
        return [[tmp[slot, c, pl.ds(r, 8, stride=4), :] for r in range(R)] for c in range(C)]

    sub_row = sublanes()
    f_d, f_x, f_y, f_s, f_i = (rows_in(fld, k, k % 3) for k in range(5))
    store_state(src, f_s)
    store_state(fbuf, f_i)
    for c in range(C):
        for r in range(R):
            d, vx, vy = f_d[c][r], f_x[c][r], f_y[c][r]
            k0 = 4.0 * d + (jnp.abs(vx) + jnp.abs(vy))
            kl = d + jnp.maximum(vx, 0.0)
            kr = d - jnp.minimum(vx, 0.0)
            ku = d + jnp.maximum(vy, 0.0)
            kd = d - jnp.minimum(vy, 0.0)
            if r == 0:
                ku = jnp.where(sub_row == 0, 0.0, ku)
            if r == R - 1:
                kd = jnp.where(sub_row == 7, 0.0, kd)
            for ref, scale in ((c1, 1.0), (c8, 8.0), (c64, 64.0)):
                ref[0, c, r] = 1.0 - scale * k0
                for k, val in enumerate((kl, kr, ku, kd)):
                    ref[k + 1, c, r] = scale * val

    own[5].wait()
    sib[5].wait_recv()
    for k in range(7):
        store_state(st, rows_in(cp, k + 2, k % 3), k)

    def pair(i, carry):
        j = 2 * i
        a, b = full_steps(M, [load_state(st, j), load_state(st, j + 1)], c1, src)
        store_state(st, a, j + 7)
        store_state(st, b, j + 8)
        return carry

    lax.fori_loop(0, 6, pair, 0)

    @pl.when(p > 0)
    def _():
        for ss in range(2):
            remote(
                tail, cp.at[pl.ds(0, 2), pl.ds(16 * ss, 16), :], dev(p, other), 6, 6 + ss
            ).wait_recv()

    first_slab = p == 0

    @pl.when(p > 0)
    def _():
        for k in range(2):
            store_state(sp, rows_in(cp, k, k), k)

    @pl.when(first_slab)
    def _():
        for k in range(2):
            store_state(sp, load_state(fbuf), k)

    a, b, e = full_steps(M, [load_state(sp, 0), load_state(sp, 1), load_state(st, 12)], c1, src)
    store_state(sp, a, 2)
    store_state(sp, b, 3)
    store_state(st, e, 19)

    @pl.when(first_slab)
    def _():
        store_state(sp, load_state(fbuf), 2)

    a, b = full_steps(M, [load_state(sp, 2), load_state(sp, 3)], c1, src)
    store_state(dfc, sub(a, load_state(sp, 3)), 0)
    store_state(dfc, sub(b, load_state(st, 7)), 1)

    def defects(k, carry):
        store_state(dfc, sub(load_state(st, 12 + k), load_state(st, 6 + k)), k)
        return carry

    lax.fori_loop(2, M, defects, 0)

    def climb(k, v):
        return add(full_step([v], c8)[0], load_state(dfc, k))

    v = lax.fori_loop(1, M, climb, load_state(dfc, 0))
    store_state(lev, v)
    level = remote(lev, lag, dev(p + 1, s), 8, 8)

    @pl.when(p < n_tm - 1)
    def _():
        level.start()

    (v,) = full_steps(M, [v], c8)

    for c, tile in enumerate(window_tiles(v, s)):
        store_win(w1s, tile, c)
    to_x = []
    for d in range(1, NX):
        xx = lax.rem(x + d, NX)
        copy = remote(w1s.at[xx], w1.at[x], dev(NX * g + xx, s), 9 + d, 9 + x)
        copy.start()
        to_x.append(copy)
    store_win(w1, load_win(w1s, x), x)
    for k in range(5):
        tiles = window_tiles(load_state(c64, k), s)
        for r in range(R):
            mine = tiles[0][r]
            for c in range(1, C):
                mine = jnp.where(x == c, tiles[c][r], mine)
            cwin[k, r] = mine
    for d in range(1, NX):
        xx = lax.rem(x + d, NX)
        remote(w1s.at[xx], w1.at[xx], dev(NX * g + xx, s), 9, 9 + xx).wait_recv()
    acc = load_win(w1, 0)
    for i in range(1, NX):
        acc = add(win_step(acc, cwin), load_win(w1, i))
    store_win(u1, acc, z)

    to_z = []
    for d in (4, 3, 5, 2, 6, 1, 7) if NZ == 8 else range(1, NZ):
        zz = lax.rem(z + d, NZ)
        copy = remote(u1.at[z], u1.at[z], dev(plane * y + NX * zz + x, s), 13 + d, 13 + z)
        copy.start()
        to_z.append(copy)
    acc = [jnp.zeros(T, jnp.float32)] * R
    for zz in range(NZ):
        @pl.when(z == zz)
        def _():
            store_win(pz, acc)

        @pl.when(z != zz)
        def _():
            remote(u1.at[zz], u1.at[zz], dev(p, other), 13, 13 + zz).wait_recv()

        if zz > 0:
            acc = win_steps(NX, acc, cwin)
        acc = add(acc, load_win(u1, zz))
    store_win(t2own, acc)
    swap_t = remote(t2own, t2sib, dev(p, other), 21, 21)
    swap_t.start()

    acc = load_win(pz)
    store_win(rown, acc, 0)
    for i in range(NX):
        acc = add(win_step(acc, cwin), load_win(w1, i))
        store_win(rown, acc, i + 1)
    swap_r = remote(rown, rsib, dev(p, other), 38, 38)
    swap_r.start()

    swap_t.wait_recv()
    store_win(t2m, merged(load_win(t2own), load_win(t2sib), s))
    to_y = []
    for yy in range(1, n_y):
        for xx in range(NX):
            copy = remote(
                t2m, t2.at[y, x], dev(plane * yy + NX * z + xx, s),
                22 + NX * yy + xx, 22 + NX * y + x,
            )
            to_y.append((yy, copy))

            @pl.when(yy > y)
            def _():
                copy.start()

    swap_r.wait_recv()
    for i in range(NX + 1):
        store_win(rm, merged(load_win(rown, i), load_win(rsib, i), s), i)
    to_r = []
    for i in range(NX):
        there = NX * g + 1 + i
        copy = remote(rm.at[pl.ds(i, 2)], rr.at[x], dev(there, s), 39 + i, 39 + x)
        go = jnp.logical_and(x != i + 1, there < n_tm) if i == NX - 1 else x != i + 1
        to_r.append((go, copy))

        @pl.when(go)
        def _():
            copy.start()

        if i < NX - 1:
            @pl.when(x == i + 1)
            def _():
                store_win(rr, load_win(rm, i), x, 0)
                store_win(rr, load_win(rm, i + 1), x, 1)

    @pl.when(first_slab)
    def _():
        zero = [jnp.zeros(T, jnp.float32)] * R
        for c in range(C):
            store_win(rr, zero, c, 0)
            store_win(rr, zero, c, 1)
            store_win(lag, zero, c)

    q = jnp.maximum(p - 1, 0)
    xq = lax.rem(q, NX)
    zq = lax.rem(lax.div(q, NX), NZ)
    yq = lax.div(q, plane)
    store_state(fbuf, [[jnp.zeros(T, jnp.float32)] * R] * C)
    for yy in range(n_y - 1):
        @pl.when(yy < y)
        def _():
            for xx in range(NX):
                remote(t2m, t2.at[yy, xx], dev(p, other), 22, 22 + NX * yy + xx).wait_recv()

        @pl.when(yy < yq)
        def _():
            f = load_state(t2, yy)
            if yy > 0:
                (old,) = full_steps(plane, [load_state(fbuf)], c64)
                f = add(old, f)
            store_state(fbuf, f)

    trips = jnp.where(yq > 0, xq + NX * zq, 0)
    (f,) = full_steps(trips, [load_state(fbuf)], c64)

    @pl.when(p > 0)
    def _():
        level.wait_recv()
        for xx in range(NX):
            @pl.when(jnp.logical_or(x == 0, x != xx))
            def _():
                remote(rm.at[pl.ds(0, 2)], rr.at[xx], dev(p, other), 39, 39 + xx).wait_recv()

    e = [add(f[c], load_win(rr, c, 0)) for c in range(C)]
    (f,) = full_step([f], c64)
    last = [add(f[c], load_win(rr, c, 1)) for c in range(C)]
    last = add(last, load_state(lev))
    walker = add(load_state(lag), e)

    def emit(k, value):
        for c in range(C):
            for r in range(R):
                tmp[0, c, pl.ds(r, 8, stride=4), :] = value[c][r]
        for c in range(C):
            for t in range(2):
                outb[k, pl.ds(8 * t, 8), COLS[c]] = tmp[0, c, pl.ds(row0 + 8 * t, 8), :]

    def errors(k, v):
        v = add(full_step([v], c8)[0], load_state(dfc, k))
        store_state(st, add(v, load_state(st, k + 6)), k + 6)
        return v

    store_state(st, load_state(sp, 3), 6)
    lax.fori_loop(0, M - 1, errors, walker)
    store_state(st, add(last, load_state(st, 13)), 13)

    def emit_k(k, carry):
        emit(k, load_state(st, k + 6))
        return carry

    lax.fori_loop(0, M, emit_k, 0)
    done = pltpu.make_async_copy(outb, out, loc.at[6])
    done.start()

    for copy in sib:
        copy.wait_send()

    @pl.when(p < n_tm - 1)
    def _():
        for copy in ahead:
            copy.wait_send()
        level.wait_send()

    for copy in to_x + to_z + [swap_t, swap_r]:
        copy.wait_send()
    for yy, copy in to_y:
        @pl.when(yy > y)
        def _():
            copy.wait_send()

    for go, copy in to_r:
        @pl.when(go)
        def _():
            copy.wait_send()

    done.wait()


def body(n_tm, *args):
    f32 = jnp.float32

    def vmem(*shape):
        return pltpu.VMEM(shape, f32)

    state = STATE
    scratch = [
        vmem(9, 32, 512), vmem(5, 32, 512),
        vmem(5, *state), vmem(5, *state), vmem(5, *state), vmem(*state), vmem(5, *WIN),
        vmem(3, C, 32, 128), vmem(20, *state), vmem(4, *state), vmem(M, *state),
        vmem(*state), vmem(*state),
        vmem(NX, *WIN), vmem(NX, *WIN), vmem(NZ, *WIN), vmem(*WIN),
        vmem(*WIN), vmem(*WIN), vmem(*WIN), vmem(max(n_tm // (NX * NZ) - 1, 1), C, *WIN),
        vmem(NX + 1, *WIN), vmem(NX + 1, *WIN), vmem(NX + 1, *WIN), vmem(C, 2, *WIN),
        vmem(*state), vmem(M, 16, 512),
        pltpu.SemaphoreType.DMA((43,)), pltpu.SemaphoreType.DMA((43,)), pltpu.SemaphoreType.DMA((7,)),
    ]
    return pl.pallas_call(
        functools.partial(kernel, n_tm),
        out_shape=jax.ShapeDtypeStruct(args[0].shape, f32),
        in_specs=[pl.BlockSpec(memory_space=pl.ANY)] * 6,
        out_specs=pl.BlockSpec(memory_space=pl.ANY),
        scratch_shapes=scratch,
        compiler_params=pltpu.CompilerParams(
            collective_id=0, has_side_effects=True, vmem_limit_bytes=32 * 1024 * 1024
        ),
    )(*args)


def solution(mesh):
    placed = (
        P("tm", "space", None),
        P("space", None),
        P("space", None),
        P("space", None),
        P("space", None),
        P("space", None),
    )
    return jax.shard_map(
        functools.partial(body, mesh.shape["tm"]),
        mesh=mesh, in_specs=placed, out_specs=P("tm", "space", None), check_vma=False,
    )
```

```python
import functools

import jax
import jax.numpy as jnp
from jax import lax
from jax.experimental import pallas as pl
from jax.experimental.pallas import tpu as pltpu
from jax.sharding import PartitionSpec as P

M = 8
NX = 4
NZ = 8
C = 4
R = 4
T = (8, 128)
W = 128 * C
NY = 8 * R
MESH = pl.DeviceIdType.MESH
BF16 = jnp.bfloat16
F32 = jnp.float32


def tile(ref, lead, r, c):
    return ref[(*lead, pl.ds(8 * r, 8), pl.ds(128 * c, 128))]


def load_state(ref, *lead, columns=C):
    return [[tile(ref, lead, r, c) for r in range(R)] for c in range(columns)]


def store_state(ref, v, *lead):
    for c, column in enumerate(v):
        for r in range(R):
            ref[(*lead, pl.ds(8 * r, 8), pl.ds(128 * c, 128))] = column[r]


def load_win(ref, *lead):
    return load_state(ref, *lead, columns=1)[0]


def store_win(ref, v, *lead):
    store_state(ref, [v], *lead)


def add(a, b):
    if isinstance(a, list):
        return [add(x, y) for x, y in zip(a, b)]
    return a + b


def sub(a, b):
    if isinstance(a, list):
        return [sub(x, y) for x, y in zip(a, b)]
    return a - b


def iota(shape, dim):
    return lax.broadcasted_iota(jnp.int32, shape, dim)


def at_row(column, r, di):
    carry, index = divmod(r + di, R)
    x = column[index]
    return x if carry == 0 else pltpu.roll(x, (-carry) % 8, 0)


def beside(v, width):
    ext = {c: v[c] for c in range(C)}
    for j in range(1, width + 1):
        ext[-j] = [pltpu.roll(x, 1, 1) for x in v[C - j]]
        ext[C - 1 + j] = [pltpu.roll(x, 127, 1) for x in v[j - 1]]
    return ext


def advance(states, coef, first, count, source=None):
    exts = [beside(v, count) for v in states]
    for j in range(count):
        width = count - 1 - j
        news = [{} for _ in exts]
        for c in range(-width, C + width):
            for n in news:
                n[c] = []
            for r in range(R):
                k0, kl, kr, ku, kd = (tile(coef, (k,), r, c - first) for k in range(5))
                plus = None if source is None else tile(source, (), r, c)
                for n, e in zip(news, exts):
                    new = (k0 * e[c][r] + kl * e[c - 1][r]) + (kr * e[c + 1][r] + ku * at_row(e[c], r, -1))
                    new = new + kd * at_row(e[c], r, 1)
                    n[c].append(new if plus is None else new + plus)
        exts = news
    return [[e[c] for c in range(C)] for e in exts]


def relax(states, coef, source):
    return lax.fori_loop(0, M, lambda _, s: advance(s, coef, 0, 1, source), states)


def move(v, coef, times, count=2, unroll=1):
    def some(_, s):
        for _ in range(unroll):
            s = advance(s, coef, -1, count)
        return s

    return lax.fori_loop(0, times, some, [v])[0]


ONE = [(0, 0), (0, -1), (0, 1), (-1, 0), (1, 0)]


def sums(a, b):
    out = []
    for d in a:
        for e in b:
            f = (d[0] + e[0], d[1] + e[1])
            if f not in out:
                out.append(f)
    return out


TWO = sums(ONE, ONE)
FOUR = sums(TWO, TWO)


def along(v, dj):
    return v if dj == 0 else [pltpu.roll(x, (-dj) % 128, 1) for x in v]


def win_apply(v, coef, offsets):
    moved = {dj: along(v, dj) for dj in sorted({d[1] for d in offsets})}
    out = []
    for r in range(R):
        parts = [None] * 4
        for n, (di, dj) in enumerate(offsets):
            term = tile(coef, (n,), r, 0) * at_row(moved[dj], r, di)
            parts[n % 4] = term if parts[n % 4] is None else parts[n % 4] + term
        out.append((parts[0] + parts[1]) + (parts[2] + parts[3]))
    return out


def compose(out, a, a_offsets, b, b_offsets, out_offsets):
    seen = set()
    for dj in sorted({d[1] for d in a_offsets}):
        for n, e in enumerate(b_offsets):
            moved = along(load_win(b, n), dj)
            for m, d in enumerate(a_offsets):
                if d[1] != dj:
                    continue
                k = out_offsets.index((d[0] + e[0], d[1] + e[1]))
                for r in range(R):
                    term = tile(a, (m,), r, 0) * at_row(moved, r, d[0])
                    if k in seen:
                        term = term + tile(out, (k,), r, 0)
                    out[k, pl.ds(8 * r, 8), :] = term
                seen.add(k)


def permuted(x, matrix):
    high = x.astype(BF16)
    rest = x - high.astype(F32)
    mid = rest.astype(BF16)
    low = (rest - mid.astype(F32)).astype(BF16)
    a, b, c = (jnp.dot(part, matrix, preferred_element_type=F32) for part in (high, mid, low))
    return (a + b) + c


def selector(row_of_column):
    return jnp.where(iota((W, W), 0) == row_of_column, 1.0, 0.0).astype(BF16)


def inner_place(column):
    return 128 * lax.rem(column, C) + lax.div(column, C)


def merged(own, other, band):
    lane = iota(T, 1)
    low = band == 0
    out = []
    for a, b in zip(own, other):
        w0, w1 = jnp.where(low, a, b), jnp.where(low, b, a)
        out.append(jnp.where(lane < 64, pltpu.roll(w0, 96, 1), pltpu.roll(w1, 32, 1)))
    return out


def kernel(
    n_tm, cpoints, initial, diffusion, velocity_x, velocity_y, source, out,
    raw, perm_in, perm_win, perm_out, c1, c8, c64, src, init, cw1, cw2, cw4, cwide, rows, cpi, rel, dfc,
    lev, lag, w1s, w1, u1, pz, t2own, t2sib, t2m, t2, rown, rsib, rm, rr, rri, t2i, fbuf, outi, outb,
    send, recv, loc,
):
    p = lax.axis_index("tm")
    s = lax.axis_index("space")
    x = lax.rem(p, NX)
    g = lax.div(p, NX)
    z = lax.rem(g, NZ)
    y = lax.div(g, NZ)
    n_y = n_tm // (NX * NZ)
    plane = NX * NZ
    other = 1 - s
    row0 = pl.multiple_of(16 * s, 16)
    first_slab = p == 0

    def dev(tm, space):
        return {"tm": tm, "space": space}

    def cols(c):
        return pl.ds(pl.multiple_of(128 * c, 128), 128)

    barrier = pltpu.get_barrier_semaphore()

    def greet(tm, space):
        pl.semaphore_signal(barrier, inc=1, device_id=dev(tm, space), device_id_type=MESH)

    for d in (4, 3, 5, 2, 6, 1, 7):
        greet(plane * y + NX * lax.rem(z + d, NZ) + x, s)
    for yy in range(n_y - 1):
        @pl.when(yy < y)
        def _():
            for xx in range(NX):
                greet(plane * yy + NX * z + xx, s)

    @pl.when(p > 0)
    def _():
        greet(p - 1, 0)
        greet(p - 1, 1)

    for d in (2, 1, 3):
        greet(NX * g + lax.rem(x + d, NX), s)

    @pl.when(jnp.logical_and(x == 0, p > 0))
    def _():
        for d in range(1, NX + 1):
            greet(p - d, s)

    greet(p, other)

    fields = (diffusion, velocity_x, velocity_y, source, initial)
    own = [pltpu.make_async_copy(f, raw.at[k, pl.ds(row0, 16), :], loc.at[k]) for k, f in enumerate(fields)]
    own.append(
        pltpu.make_async_copy(cpoints.at[pl.ds(0, 7)], raw.at[pl.ds(5, 7), pl.ds(row0, 16), :], loc.at[5])
    )
    for copy in own:
        copy.start()

    sends = 1 + (NX - 1) + (NZ - 1) + NX * (n_y - 1 - y)
    sends = sends + jnp.where(p < n_tm - 1, 2, 0)
    sends = sends + jnp.where(g < n_tm // NX - 1, 1, 0)
    pl.semaphore_wait(barrier, sends)

    def remote(src_ref, dst_ref, to, send_idx, recv_idx):
        return pltpu.make_async_remote_copy(
            src_ref=src_ref, dst_ref=dst_ref, send_sem=send.at[send_idx], recv_sem=recv.at[recv_idx],
            device_id=to, device_id_type=MESH,
        )

    tail = cpoints.at[pl.ds(6, 2)]
    ahead = [
        remote(tail, raw.at[pl.ds(12, 2), pl.ds(row0, 16), :], dev(p + 1, ss), 6 + ss, 6 + s) for ss in range(2)
    ]

    @pl.when(p < n_tm - 1)
    def _():
        for copy in ahead:
            copy.start()

    sib = [
        remote(f, raw.at[k, pl.ds(row0, 16), :], dev(p, other), k, k) for k, f in enumerate(fields)
    ]
    sib.append(
        remote(cpoints.at[pl.ds(0, 7)], raw.at[pl.ds(5, 7), pl.ds(row0, 16), :], dev(p, other), 5, 5)
    )
    for copy in sib:
        copy.start()

    line = iota((1, W), 1)
    perm_in[...] = selector(C * lax.rem(line, 128) + lax.div(line, 128))

    for copy in own:
        copy.wait()
    for copy in sib:
        copy.wait_recv()

    def inward(first, count, emit):
        moved = permuted(raw[pl.ds(first, count)].reshape(count * NY, W), perm_in[...])
        for c in range(C):
            rows[c, pl.ds(0, count * NY), :] = moved[:, 128 * c : 128 * (c + 1)]
        for k in range(count):
            emit(k, [[rows[c, pl.ds(NY * k + r, 8, stride=R), :] for r in range(R)] for c in range(C)])

    got = {}

    def keep(k, v):
        if k < 3:
            got[k] = v
        elif k == 3:
            store_state(src, v)
        elif k == 4:
            store_state(init, v)
        else:
            store_state(cpi, v, k - 3)

    inward(0, 12, keep)

    sub_row = iota(T, 0)
    for c in range(C):
        for r in range(R):
            d, vx, vy = (got[k][c][r] for k in range(3))
            k0 = 4.0 * d + (jnp.abs(vx) + jnp.abs(vy))
            kl = d + jnp.maximum(vx, 0.0)
            kr = d - jnp.minimum(vx, 0.0)
            ku = d + jnp.maximum(vy, 0.0)
            kd = d - jnp.minimum(vy, 0.0)
            if r == 0:
                ku = jnp.where(sub_row == 0, 0.0, ku)
            if r == R - 1:
                kd = jnp.where(sub_row == 7, 0.0, kd)
            here = (pl.ds(8 * r, 8), pl.ds(128 * c, 128))
            wide = (pl.ds(8 * r, 8), pl.ds(128 * (c + 1), 128))
            for ref, scale, at in ((c1, 1.0, here), (c8, 8.0, wide), (c64, 64.0, wide)):
                ref[(0, *at)] = 1.0 - scale * k0
                for k, val in enumerate((kl, kr, ku, kd)):
                    ref[(k + 1, *at)] = scale * val

    first = relax([load_state(cpi, k) for k in range(2, 9)], c1, src)
    for k, v in enumerate(first):
        store_state(rel, v, k + 2)

    @pl.when(p > 0)
    def _():
        for ss in range(2):
            remote(
                tail, raw.at[pl.ds(12, 2), pl.ds(16 * ss, 16), :], dev(p, other), 6, 6 + ss
            ).wait_recv()

        inward(12, 2, lambda k, v: store_state(cpi, v, k))

    @pl.when(first_slab)
    def _():
        for k in range(2):
            store_state(cpi, load_state(init), k)

    second = relax(
        [load_state(cpi, 0), load_state(cpi, 1)] + [load_state(rel, k) for k in range(2, 8)], c1, src
    )
    for k in range(2):
        store_state(rel, second[k], k)
    for k in range(2, M):
        store_state(dfc, sub(second[k], load_state(rel, k + 1)), k)

    @pl.when(first_slab)
    def _():
        store_state(rel, load_state(init), 0)

    third = relax([load_state(rel, 0), load_state(rel, 1)], c1, src)
    for k in range(2):
        store_state(dfc, sub(third[k], load_state(rel, k + 1)), k)

    for ref in (c8, c64):
        for k in range(5):
            for r in range(R):
                ref[k, pl.ds(8 * r, 8), pl.ds(0, 128)] = pltpu.roll(tile(ref, (k,), r, C), 1, 1)
                ref[k, pl.ds(8 * r, 8), pl.ds(128 * (C + 1), 128)] = pltpu.roll(tile(ref, (k,), r, 1), 127, 1)

    def climb(k, v):
        return add(advance([v], c8, -1, 1)[0], load_state(dfc, k))

    v = lax.fori_loop(1, M, climb, load_state(dfc, 0))
    store_state(lev, v)
    level = remote(lev, lag, dev(p + 1, s), 8, 8)
    v = move(v, c8, M // 2)
    store_state(fbuf, v)

    perm_win[...] = selector(
        inner_place(lax.rem(128 * lax.div(line, 128) + 64 * s + (W - 32) + lax.rem(line, 128), W))
    )
    w1s[...] = permuted(fbuf[...], perm_win[...])
    to_x = []
    for d in (2, 1, 3):
        xx = lax.rem(x + d, NX)
        copy = remote(w1s.at[:, cols(xx)], w1.at[x], dev(NX * g + xx, s), 9 + d, 9 + x)
        copy.start()
        to_x.append(copy)

    @pl.when(p < n_tm - 1)
    def _():
        level.start()

    store_win(w1, [w1s[pl.ds(8 * r, 8), cols(x)] for r in range(R)], x)

    cwide[...] = permuted(c64[:, :, pl.ds(128, W)].reshape(5 * NY, W), perm_win[...])
    for k in range(5):
        cw1[k] = cwide[pl.ds(NY * k, NY), cols(x)]
    compose(cw2, cw1, ONE, cw1, ONE, TWO)
    compose(cw4, cw2, TWO, cw2, TWO, FOUR)
    perm_out[...] = selector(inner_place(line))

    for d in range(1, NX):
        xx = lax.rem(x + d, NX)
        remote(w1s.at[:, cols(xx)], w1.at[xx], dev(NX * g + xx, s), 9, 9 + xx).wait_recv()
    a = add(win_apply(load_win(w1, 0), cw1, ONE), load_win(w1, 1))
    b = add(win_apply(load_win(w1, 2), cw1, ONE), load_win(w1, 3))
    store_win(u1, add(win_apply(a, cw2, TWO), b), z)

    to_z = []
    for d in (4, 3, 5, 2, 6, 1, 7):
        zz = lax.rem(z + d, NZ)
        copy = remote(u1.at[z], u1.at[z], dev(plane * y + NX * zz + x, s), 13 + d, 13 + z)
        copy.start()
        to_z.append(copy)

    pz[...] = jnp.zeros_like(pz)

    @pl.when(z != 0)
    def _():
        remote(u1.at[0], u1.at[0], dev(p, other), 13, 13).wait_recv()

    def ascend(zz, acc):
        @pl.when(z == zz)
        def _():
            store_win(pz, acc)

        @pl.when(z != zz)
        def _():
            remote(u1.at[zz], u1.at[zz], dev(p, other), 13, 13 + zz).wait_recv()

        return add(win_apply(acc, cw4, FOUR), load_win(u1, zz))

    store_win(t2own, lax.fori_loop(1, NZ, ascend, load_win(u1, 0)))
    swap_t = remote(t2own, t2sib, dev(p, other), 21, 21)
    swap_t.start()

    acc = load_win(pz)
    store_win(rown, acc, 0)
    for i in range(NX):
        acc = add(win_apply(acc, cw1, ONE), load_win(w1, i))
        store_win(rown, acc, i + 1)
    swap_r = remote(rown, rsib, dev(p, other), 38, 38)
    swap_r.start()

    swap_t.wait_recv()
    store_win(t2m, merged(load_win(t2own), load_win(t2sib), s))
    to_y = []
    for yy in range(1, n_y):
        for xx in range(NX):
            copy = remote(
                t2m, t2.at[y, :, cols(x)], dev(plane * yy + NX * z + xx, s),
                22 + NX * yy + xx, 22 + NX * y + x,
            )
            to_y.append((yy, copy))

            @pl.when(yy > y)
            def _():
                copy.start()

    swap_r.wait_recv()
    for i in range(NX + 1):
        store_win(rm, merged(load_win(rown, i), load_win(rsib, i), s), i)
    to_r = []
    for i in range(NX):
        there = NX * g + 1 + i
        copy = remote(rm.at[pl.ds(i, 2)], rr.at[:, :, cols(x)], dev(there, s), 39 + i, 39 + x)
        go = jnp.logical_and(x != i + 1, there < n_tm) if i == NX - 1 else x != i + 1
        to_r.append((go, copy))

        @pl.when(go)
        def _():
            copy.start()

        if i < NX - 1:
            @pl.when(x == i + 1)
            def _():
                for j in range(2):
                    rr[j, :, cols(x)] = rm[i + j]

    @pl.when(first_slab)
    def _():
        rr[...] = jnp.zeros_like(rr)
        lag[...] = jnp.zeros_like(lag)

    @pl.when(p > 0)
    def _():
        level.wait_recv()
        for xx in range(NX):
            @pl.when(jnp.logical_or(x == 0, x != xx))
            def _():
                remote(
                    rm.at[pl.ds(0, 2)], rr.at[:, :, cols(xx)], dev(p, other), 39, 39 + xx
                ).wait_recv()

    rri[...] = permuted(rr[...].reshape(2 * NY, W), perm_in[...]).reshape(2, NY, W)

    q = jnp.maximum(p - 1, 0)
    n = lax.rem(q, plane)
    yq = lax.div(q, plane)
    fbuf[...] = jnp.zeros_like(fbuf)
    for yy in range(n_y - 1):
        @pl.when(yy < y)
        def _():
            for xx in range(NX):
                remote(t2m, t2.at[yy, :, cols(xx)], dev(p, other), 22, 22 + NX * yy + xx).wait_recv()

    for yy in range(n_y - 1):
        @pl.when(yy < yq)
        def _():
            t2i[...] = permuted(t2[yy], perm_in[...])
            f = load_state(t2i)
            if yy > 0:
                f = add(move(load_state(fbuf), c64, plane // 4, 2, 2), f)
            store_state(fbuf, f)

    n = jnp.where(yq > 0, n, 0)
    f = move(load_state(fbuf), c64, lax.div(n, 2))
    f = move(f, c64, lax.rem(n, 2), 1)
    e = add(f, load_state(rri, 0))
    (f,) = advance([f], c64, -1, 1)
    last = add(add(f, load_state(rri, 1)), load_state(lev))

    def emit(k, value):
        for c in range(C):
            for r in range(R):
                rows[c, pl.ds(r, 8, stride=R), :] = value[c][r]
        for c in range(C):
            for t in range(2):
                outi[k, pl.ds(8 * t, 8), pl.ds(128 * c, 128)] = rows[c, pl.ds(pl.multiple_of(row0 + 8 * t, 8), 8), :]

    emit(M - 1, add(last, load_state(rel, M)))

    def errors(k, v):
        v = add(advance([v], c8, -1, 1)[0], load_state(dfc, k))
        emit(k, add(v, load_state(rel, k + 1)))
        return v

    lax.fori_loop(0, M - 1, errors, add(load_state(lag), e))
    outb[...] = permuted(outi[...].reshape(M * 16, W), perm_out[...]).reshape(M, 16, W)
    done = pltpu.make_async_copy(outb, out, loc.at[6])
    done.start()

    for copy in sib:
        copy.wait_send()

    @pl.when(p < n_tm - 1)
    def _():
        for copy in ahead:
            copy.wait_send()
        level.wait_send()

    for copy in to_x + to_z + [swap_t, swap_r]:
        copy.wait_send()
    for yy, copy in to_y:
        @pl.when(yy > y)
        def _():
            copy.wait_send()

    for go, copy in to_r:
        @pl.when(go)
        def _():
            copy.wait_send()

    done.wait()


def body(n_tm, *args):
    def vmem(*shape, dtype=F32):
        return pltpu.VMEM(shape, dtype)

    def state(*lead):
        return vmem(*lead, NY, W)

    def window(*lead):
        return vmem(*lead, NY, 128)

    square = vmem(W, W, dtype=BF16)
    scratch = [
        state(14), square, square, square,
        state(5), vmem(5, NY, W + 256), vmem(5, NY, W + 256), state(), state(),
        window(len(ONE)), window(len(TWO)), window(len(FOUR)), vmem(5 * NY, W),
        vmem(C, 12 * NY, 128), state(9), state(9), state(M),
        state(), state(), state(), window(NX), window(NZ), window(),
        window(), window(), window(), state(max(n_tm // (NX * NZ) - 1, 1)),
        window(NX + 1), window(NX + 1), window(NX + 1), state(2), state(2), state(),
        state(), vmem(M, 16, W), vmem(M, 16, W),
        pltpu.SemaphoreType.DMA((43,)), pltpu.SemaphoreType.DMA((43,)), pltpu.SemaphoreType.DMA((7,)),
    ]
    return pl.pallas_call(
        functools.partial(kernel, n_tm),
        out_shape=jax.ShapeDtypeStruct(args[0].shape, F32),
        in_specs=[pl.BlockSpec(memory_space=pltpu.HBM)] * 6,
        out_specs=pl.BlockSpec(memory_space=pltpu.HBM),
        scratch_shapes=scratch,
        compiler_params=pltpu.CompilerParams(
            collective_id=0, has_side_effects=True, vmem_limit_bytes=40 * 1024 * 1024
        ),
    )(*args)


def solution(mesh):
    placed = (
        P("tm", "space", None),
        P("space", None),
        P("space", None),
        P("space", None),
        P("space", None),
        P("space", None),
    )
    return jax.shard_map(
        functools.partial(body, mesh.shape["tm"]),
        mesh=mesh, in_specs=placed, out_specs=P("tm", "space", None), check_vma=False,
    )
```

```python
import functools

import jax
import jax.numpy as jnp
from jax import lax
from jax.experimental import pallas as pl
from jax.experimental.pallas import tpu as pltpu
from jax.sharding import PartitionSpec as P

M = 8
NX = 4
NZ = 8
C = 4
R = 4
T = (8, 128)
W = 128 * C
NY = 8 * R
MESH = pl.DeviceIdType.MESH
BF16 = jnp.bfloat16
F32 = jnp.float32


def tile(ref, lead, r, c):
    return ref[(*lead, pl.ds(8 * r, 8), pl.ds(128 * c, 128))]


def load_state(ref, *lead, columns=C):
    return [[tile(ref, lead, r, c) for r in range(R)] for c in range(columns)]


def store_state(ref, v, *lead):
    for c, column in enumerate(v):
        for r in range(R):
            ref[(*lead, pl.ds(8 * r, 8), pl.ds(128 * c, 128))] = column[r]


def load_win(ref, *lead):
    return load_state(ref, *lead, columns=1)[0]


def store_win(ref, v, *lead):
    store_state(ref, [v], *lead)


def add(a, b):
    if isinstance(a, list):
        return [add(x, y) for x, y in zip(a, b)]
    return a + b


def sub(a, b):
    if isinstance(a, list):
        return [sub(x, y) for x, y in zip(a, b)]
    return a - b


def iota(shape, dim):
    return lax.broadcasted_iota(jnp.int32, shape, dim)


def at_row(column, r, di):
    carry, index = divmod(r + di, R)
    x = column[index]
    return x if carry == 0 else pltpu.roll(x, (-carry) % 8, 0)


def beside(v, width):
    ext = {c: v[c] for c in range(C)}
    for j in range(1, width + 1):
        ext[-j] = [pltpu.roll(x, 1, 1) for x in v[C - j]]
        ext[C - 1 + j] = [pltpu.roll(x, 127, 1) for x in v[j - 1]]
    return ext


def advance(states, coef, first, count, source=None):
    exts = [beside(v, count) for v in states]
    for j in range(count):
        width = count - 1 - j
        news = [{} for _ in exts]
        for c in range(-width, C + width):
            for n in news:
                n[c] = []
            for r in range(R):
                k0, kl, kr, ku, kd = (tile(coef, (k,), r, c - first) for k in range(5))
                plus = None if source is None else tile(source, (), r, c)
                for n, e in zip(news, exts):
                    new = (k0 * e[c][r] + kl * e[c - 1][r]) + (kr * e[c + 1][r] + ku * at_row(e[c], r, -1))
                    new = new + kd * at_row(e[c], r, 1)
                    n[c].append(new if plus is None else new + plus)
        exts = news
    return [[e[c] for c in range(C)] for e in exts]


def relax(states, coef, source):
    return lax.fori_loop(0, M, lambda _, s: advance(s, coef, 0, 1, source), states)


def move(v, coef, times, count=2, unroll=1):
    def some(_, s):
        for _ in range(unroll):
            s = advance(s, coef, -1, count)
        return s

    return lax.fori_loop(0, times, some, [v])[0]


ONE = [(0, 0), (0, -1), (0, 1), (-1, 0), (1, 0)]


def sums(a, b):
    out = []
    for d in a:
        for e in b:
            f = (d[0] + e[0], d[1] + e[1])
            if f not in out:
                out.append(f)
    return out


TWO = sums(ONE, ONE)
FOUR = sums(TWO, TWO)


def along(v, dj):
    return v if dj == 0 else [pltpu.roll(x, (-dj) % 128, 1) for x in v]


def win_apply(v, coef, offsets):
    moved = {dj: along(v, dj) for dj in sorted({d[1] for d in offsets})}
    out = []
    for r in range(R):
        parts = [None] * 4
        for n, (di, dj) in enumerate(offsets):
            term = tile(coef, (n,), r, 0) * at_row(moved[dj], r, di)
            parts[n % 4] = term if parts[n % 4] is None else parts[n % 4] + term
        out.append((parts[0] + parts[1]) + (parts[2] + parts[3]))
    return out


def compose(out, a, a_offsets, b, b_offsets, out_offsets):
    seen = set()
    for dj in sorted({d[1] for d in a_offsets}):
        for n, e in enumerate(b_offsets):
            moved = along(load_win(b, n), dj)
            for m, d in enumerate(a_offsets):
                if d[1] != dj:
                    continue
                k = out_offsets.index((d[0] + e[0], d[1] + e[1]))
                for r in range(R):
                    term = tile(a, (m,), r, 0) * at_row(moved, r, d[0])
                    if k in seen:
                        term = term + tile(out, (k,), r, 0)
                    out[k, pl.ds(8 * r, 8), :] = term
                seen.add(k)


def permuted(x, matrix):
    high = x.astype(BF16)
    rest = x - high.astype(F32)
    mid = rest.astype(BF16)
    low = (rest - mid.astype(F32)).astype(BF16)
    count = x.shape[0]
    parts = jnp.concatenate([high, mid, low], axis=0)
    out = jnp.dot(parts, matrix, preferred_element_type=F32)
    return (out[:count] + out[count : 2 * count]) + out[2 * count :]


def selector(row_of_column):
    return jnp.where(iota((W, W), 0) == row_of_column, 1.0, 0.0).astype(BF16)


def inner_place(column):
    return 128 * lax.rem(column, C) + lax.div(column, C)


def merged(own, other, band):
    lane = iota(T, 1)
    low = band == 0
    out = []
    for a, b in zip(own, other):
        w0, w1 = jnp.where(low, a, b), jnp.where(low, b, a)
        out.append(jnp.where(lane < 64, pltpu.roll(w0, 96, 1), pltpu.roll(w1, 32, 1)))
    return out


def kernel(
    n_tm, cpoints, initial, diffusion, velocity_x, velocity_y, source, out,
    raw, perm_in, perm_win, perm_out, c1, c8, c64, src, init, cw1, cw2, cw4, cwide, rows, cpi, rel, prl, relm, dfc,
    u_own, u_sib, u_sum, up, term, mid, lag, w1s, w1, u1, pz, t2own, t2sib, t2m, t2, rown, rsib, rm, rr, rri, t2i,
    fbuf, outi, outb, send, recv, loc,
):
    p = lax.axis_index("tm")
    s = lax.axis_index("space")
    x = lax.rem(p, NX)
    g = lax.div(p, NX)
    z = lax.rem(g, NZ)
    y = lax.div(g, NZ)
    n_y = n_tm // (NX * NZ)
    plane = NX * NZ
    other = 1 - s
    row0 = pl.multiple_of(16 * s, 16)
    band = pl.ds(row0, 16)
    base = 4 * s
    first_slab = p == 0

    def dev(tm, space):
        return {"tm": tm, "space": space}

    def cols(c):
        return pl.ds(pl.multiple_of(128 * c, 128), 128)

    barrier = pltpu.get_barrier_semaphore()

    def greet(tm, space):
        pl.semaphore_signal(barrier, inc=1, device_id=dev(tm, space), device_id_type=MESH)

    greet(p, other)
    for d in (4, 3, 5, 2, 6, 1, 7):
        greet(plane * y + NX * lax.rem(z + d, NZ) + x, s)
    for yy in range(n_y - 1):
        @pl.when(yy < y)
        def _():
            for xx in range(NX):
                greet(plane * yy + NX * z + xx, s)

    for d in (2, 1, 3):
        greet(NX * g + lax.rem(x + d, NX), s)
        greet(NX * g + lax.rem(x + d, NX), other)

    @pl.when(p > 0)
    def _():
        greet(p - 1, 0)
        greet(p - 1, 1)

    @pl.when(jnp.logical_and(x < 2, g > 0))
    def _():
        for xx in range(NX):
            greet(NX * (g - 1) + xx, s)

    fields = (diffusion, velocity_x, velocity_y, source, initial)
    for k, f in enumerate(fields):
        pltpu.make_async_copy(f, raw.at[k, band, :], loc.at[0]).start()
    pltpu.make_async_copy(cpoints.at[pl.ds(base, 4)], raw.at[pl.ds(5, 4), band, :], loc.at[0]).start()

    sends = 1 + 2 * (NX - 1) + (NZ - 1) + NX * (n_y - 1 - y)
    sends = sends + jnp.where(p < n_tm - 1, 2, 0) + jnp.where(g < n_tm // NX - 1, 2, 0)
    pl.semaphore_wait(barrier, sends)

    def remote(src_ref, dst_ref, to, send_idx, recv_idx):
        return pltpu.make_async_remote_copy(
            src_ref=src_ref, dst_ref=dst_ref, send_sem=send.at[send_idx], recv_sem=recv.at[recv_idx],
            device_id=to, device_id_type=MESH,
        )

    def whole(ref, idx):
        return remote(ref, ref, dev(p, other), idx, idx)

    for k, f in enumerate(fields):
        remote(f, raw.at[k, band, :], dev(p, other), 0, 0).start()
    remote(cpoints.at[pl.ds(4 * other, 4)], raw.at[pl.ds(5, 4), band, :], dev(p, other), 0, 0).start()
    sib = whole(raw.at[pl.ds(0, 9), band, :], 0)

    @pl.when(p < n_tm - 1)
    def _():
        for ss in range(2):
            remote(cpoints.at[pl.ds(6, 2)], raw.at[pl.ds(9, 2), band, :], dev(p + 1, ss), 1, 1).start()

    ahead = whole(raw.at[pl.ds(9, 2)], 1)

    line = iota((1, W), 1)
    perm_in[...] = selector(C * lax.rem(line, 128) + lax.div(line, 128))
    for ss in range(2):
        begin = 128 * lax.div(line, 128) + (64 * ss + W - 32)
        perm_win[:, pl.ds(W * ss, W)] = selector(inner_place(lax.rem(begin + lax.rem(line, 128), W)))

    pltpu.make_async_copy(raw.at[pl.ds(0, 9), band, :], raw.at[pl.ds(0, 9), band, :], loc.at[0]).wait()
    sib.wait_recv()

    def inward(first, count, emit):
        moved = permuted(raw[pl.ds(first, count)].reshape(count * NY, W), perm_in[...])
        for c in range(C):
            rows[c, pl.ds(0, count * NY), :] = moved[:, 128 * c : 128 * (c + 1)]
        for k in range(count):
            emit(k, [[rows[c, pl.ds(NY * k + r, 8, stride=R), :] for r in range(R)] for c in range(C)])

    got = {}

    def keep(k, v):
        if k < 3:
            got[k] = v
        elif k == 3:
            store_state(src, v)
        elif k == 4:
            store_state(init, v)
        else:
            store_state(cpi, v, k - 5)

    inward(0, 9, keep)

    sub_row = iota(T, 0)
    for c in range(C):
        for r in range(R):
            d, vx, vy = (got[k][c][r] for k in range(3))
            k0 = 4.0 * d + (jnp.abs(vx) + jnp.abs(vy))
            kl = d + jnp.maximum(vx, 0.0)
            kr = d - jnp.minimum(vx, 0.0)
            ku = d + jnp.maximum(vy, 0.0)
            kd = d - jnp.minimum(vy, 0.0)
            if r == 0:
                ku = jnp.where(sub_row == 0, 0.0, ku)
            if r == R - 1:
                kd = jnp.where(sub_row == 7, 0.0, kd)
            here = (pl.ds(8 * r, 8), pl.ds(128 * c, 128))
            wide = (pl.ds(8 * r, 8), pl.ds(128 * (c + 1), 128))
            for ref, scale, at in ((c1, 1.0, here), (c8, 8.0, wide), (c64, 64.0, wide)):
                ref[(0, *at)] = 1.0 - scale * k0
                for k, val in enumerate((kl, kr, ku, kd)):
                    ref[(k + 1, *at)] = scale * val

    for ref in (c8, c64):
        for k in range(5):
            for r in range(R):
                ref[k, pl.ds(8 * r, 8), pl.ds(0, 128)] = pltpu.roll(tile(ref, (k,), r, C), 1, 1)
                ref[k, pl.ds(8 * r, 8), pl.ds(128 * (C + 1), 128)] = pltpu.roll(tile(ref, (k,), r, 1), 127, 1)

    def relax_own(extra):
        once = relax([load_state(cpi, k) for k in range(4)] + extra, c1, src)
        for k in range(4):
            store_state(rel, once[k], base + 1 + k)
        twice = relax(once, c1, src)
        for k in range(4):
            store_state(prl, twice[k], base + 1 + k)
        if extra:
            store_state(mid, twice[4])

    opens = jnp.logical_and(first_slab, s == 0)

    @pl.when(opens)
    def _():
        relax_own([load_state(init)])

    @pl.when(jnp.logical_not(opens))
    def _():
        relax_own([])
        mid[...] = jnp.zeros_like(mid)

    head = sub(load_state(mid), load_state(rel, base + 1))

    def defect(k):
        return sub(load_state(prl, base + k - 1), load_state(rel, base + k))

    head, late = advance([head, defect(4)], c8, -1, 1)
    head = add(head, defect(2))
    late = add(late, load_state(prl, base + 4))
    (head,) = advance([head], c8, -1, 1)
    store_state(fbuf, add(head, defect(3)))
    store_state(term, late)

    @pl.when(s == 0)
    def _():
        v = move(load_state(fbuf), c8, 1)
        v = move(add(v, load_state(term)), c8, 5)
        store_state(u_own, v)
        store_state(term, advance([v], c64, -1, 1)[0])

    @pl.when(s == 1)
    def _():
        a, b = lax.fori_loop(
            0, 4, lambda _, v: advance(v, c8, -1, 2), [load_state(fbuf), load_state(term)]
        )
        store_state(u_own, a)
        b = move(b, c8, 3)
        store_state(term, add(advance([a], c64, -1, 1)[0], b))

    w1s[...] = permuted(term[...], perm_win[...])
    for d in (2, 1, 3, 0):
        for flip in (0, 1):
            if d == 0 and flip == 0:
                continue
            xx, ss = lax.rem(x + d, NX), lax.rem(s + flip, 2)
            remote(w1s.at[:, cols(NX * ss + xx)], w1.at[2 * x + s], dev(NX * g + xx, ss), 2, 2).start()
    to_x = whole(w1.at[pl.ds(0, 2 * NX - 1)], 2)
    own = cols(NX * s + x)
    store_win(w1, [w1s[pl.ds(8 * r, 8), own] for r in range(R)], 2 * x + s)

    half = pl.ds(base + 1, 4)
    remote(u_own, u_sib, dev(p, other), 3, 3).start()
    remote(rel.at[half], rel.at[half], dev(p, other), 3, 3).start()
    remote(prl.at[half], prl.at[half], dev(p, other), 3, 3).start()
    shared = whole(rel, 3)

    cwide[...] = permuted(
        c64[:, :, pl.ds(128, W)].reshape(5 * NY, W), perm_win[:, pl.ds(pl.multiple_of(W * s, W), W)]
    )
    for k in range(5):
        cw1[k] = cwide[pl.ds(NY * k, NY), cols(x)]
    compose(cw2, cw1, ONE, cw1, ONE, TWO)
    compose(cw4, cw2, TWO, cw2, TWO, FOUR)

    to_x.wait_recv()

    def group_term(i):
        return add(load_win(w1, 2 * i), load_win(w1, 2 * i + 1))

    a = add(win_apply(group_term(0), cw1, ONE), group_term(1))
    b = add(win_apply(group_term(2), cw1, ONE), group_term(3))
    store_win(u1, add(win_apply(a, cw2, TWO), b), z)

    for d in (4, 3, 5, 2, 6, 1, 7):
        zz = lax.rem(z + d, NZ)
        remote(u1.at[z], u1.at[z], dev(plane * y + NX * zz + x, s), 4, 16 + z).start()
    to_z = whole(u1.at[pl.ds(0, NZ - 1)], 4)

    perm_out[...] = selector(inner_place(line))
    shared.wait_recv()
    store_state(u_sum, add(load_state(u_own), load_state(u_sib)))
    to_up = remote(u_sum, up, dev(p + 1, s), 5, 5)

    @pl.when(p < n_tm - 1)
    def _():
        to_up.start()

    @pl.when(p > 0)
    def _():
        ahead.wait_recv()
        inward(9, 2, lambda k, v: store_state(cpi, v, k))

    @pl.when(first_slab)
    def _():
        up[...] = jnp.zeros_like(up)
        for k in range(2):
            store_state(cpi, load_state(init), k)

    v = relax([load_state(cpi, 0), load_state(cpi, 1)], c1, src)
    store_state(relm, v[0])
    store_state(rel, v[1], 0)

    @pl.when(first_slab)
    def _():
        store_state(relm, load_state(init))

    v = relax([load_state(relm), load_state(rel, 0)], c1, src)
    store_state(dfc, sub(v[0], load_state(rel, 0)), 0)
    store_state(prl, v[1], 0)

    def climb(k, v):
        d = sub(load_state(prl, k - 1), load_state(rel, k))
        store_state(dfc, d, k)
        return add(advance([v], c8, -1, 1)[0], d)

    v = lax.fori_loop(1, M, climb, load_state(dfc, 0))

    store_state(mid, v)

    pz[...] = jnp.zeros_like(pz)

    @pl.when(z != 0)
    def _():
        remote(u1.at[0], u1.at[0], dev(p, other), 4, 16).wait_recv()

    def ascend(zz, acc):
        @pl.when(z == zz)
        def _():
            store_win(pz, acc)

        @pl.when(z != zz)
        def _():
            remote(u1.at[zz], u1.at[zz], dev(p, other), 4, 16 + zz).wait_recv()

        return add(win_apply(acc, cw4, FOUR), load_win(u1, zz))

    store_win(t2own, lax.fori_loop(1, NZ, ascend, load_win(u1, 0)))
    swap_t = remote(t2own, t2sib, dev(p, other), 7, 7)
    swap_t.start()

    acc = load_win(pz)
    store_win(rown, acc, 0)
    for i in range(NX):
        acc = add(win_apply(acc, cw1, ONE), group_term(i))
        store_win(rown, acc, i + 1)
    swap_r = remote(rown, rsib, dev(p, other), 8, 8)
    swap_r.start()

    swap_t.wait_recv()
    store_win(t2m, merged(load_win(t2own), load_win(t2sib), s))
    for yy in range(1, n_y):
        @pl.when(yy > y)
        def _():
            for xx in range(NX):
                remote(
                    t2m, t2.at[y, :, cols(x)], dev(plane * yy + NX * z + xx, s), 8 + yy, 10 + y
                ).start()

    swap_r.wait_recv()
    for i in range(NX + 1):
        store_win(rm, merged(load_win(rown, i), load_win(rsib, i), s), i)
    to_r = []
    for i in range(NX):
        there = NX * g + 2 + i
        copy = remote(rm.at[pl.ds(i, 2)], rr.at[:, :, cols(x)], dev(there, s), 12 + i, 9)
        go = x != i + 2 if i < 2 else there < n_tm
        to_r.append((go, copy))

        @pl.when(go)
        def _():
            copy.start()

        if i < 2:
            @pl.when(x == i + 2)
            def _():
                for j in range(2):
                    rr[j, :, cols(x)] = rm[i + j]

    @pl.when(p > 0)
    def _():
        to_up.wait_recv()

    store_state(mid, add(load_state(mid), load_state(up)))
    to_lag = remote(mid, lag, dev(p + 1, s), 6, 6)

    @pl.when(p < n_tm - 1)
    def _():
        to_lag.start()

    @pl.when(p < 2)
    def _():
        rr[...] = jnp.zeros_like(rr)

    @pl.when(first_slab)
    def _():
        lag[...] = jnp.zeros_like(lag)

    @pl.when(x >= 2)
    def _():
        whole(rr.at[:, :, pl.ds(0, W - 128)], 9).wait_recv()

    @pl.when(jnp.logical_and(x < 2, g > 0))
    def _():
        whole(rr, 9).wait_recv()

    rri[...] = permuted(rr[...].reshape(2 * NY, W), perm_in[...]).reshape(2, NY, W)

    q = jnp.maximum(p - 2, 0)
    n = lax.rem(q, plane)
    yq = lax.div(q, plane)
    fbuf[...] = jnp.zeros_like(fbuf)
    for yy in range(n_y - 1):
        @pl.when(yy < y)
        def _():
            whole(t2.at[yy], 10 + yy).wait_recv()

    t2i[...] = permuted(t2[...].reshape((n_y - 1) * NY, W), perm_in[...]).reshape(n_y - 1, NY, W)
    for yy in range(n_y - 1):
        @pl.when(yy < yq)
        def _():
            f = load_state(t2i, yy)
            if yy > 0:
                f = add(move(load_state(fbuf), c64, plane // 8, 2, 4), f)
            store_state(fbuf, f)

    n = jnp.where(yq > 0, n, 0)
    f = move(load_state(fbuf), c64, lax.div(n, 2))
    f = move(f, c64, lax.rem(n, 2), 1)
    e = add(f, load_state(rri, 0))
    (f,) = advance([f], c64, -1, 1)
    last = add(add(f, load_state(rri, 1)), load_state(mid))

    def emit(k, value):
        for c in range(C):
            for r in range(R):
                rows[c, pl.ds(r, 8, stride=R), :] = value[c][r]
        for c in range(C):
            for t in range(2):
                outi[k, pl.ds(8 * t, 8), pl.ds(128 * c, 128)] = rows[c, pl.ds(pl.multiple_of(row0 + 8 * t, 8), 8), :]

    emit(M - 1, add(last, load_state(rel, M - 1)))

    def errors(k, v):
        v = add(advance([v], c8, -1, 1)[0], load_state(dfc, k))
        emit(k, add(v, load_state(rel, k)))
        return v

    @pl.when(p > 0)
    def _():
        to_lag.wait_recv()

    lax.fori_loop(0, M - 1, errors, add(load_state(lag), e))
    outb[...] = permuted(outi[...].reshape(M * 16, W), perm_out[...]).reshape(M, 16, W)
    done = pltpu.make_async_copy(outb, out, loc.at[1])
    done.start()

    sib.wait_send()

    @pl.when(p < n_tm - 1)
    def _():
        ahead.wait_send()
        to_up.wait_send()
        to_lag.wait_send()

    for copy in (to_x, shared, to_z, swap_t, swap_r):
        copy.wait_send()
    for yy in range(1, n_y):
        @pl.when(yy > y)
        def _():
            whole(t2.at[0], 8 + yy).wait_send()

    for go, copy in to_r:
        @pl.when(go)
        def _():
            copy.wait_send()

    done.wait()


def body(n_tm, *args):
    def vmem(*shape, dtype=F32):
        return pltpu.VMEM(shape, dtype)

    def state(*lead):
        return vmem(*lead, NY, W)

    def window(*lead):
        return vmem(*lead, NY, 128)

    square = vmem(W, W, dtype=BF16)
    scratch = [
        state(11), square, vmem(W, 2 * W, dtype=BF16), square,
        state(5), vmem(5, NY, W + 256), vmem(5, NY, W + 256), state(), state(),
        window(len(ONE)), window(len(TWO)), window(len(FOUR)), vmem(5 * NY, W),
        vmem(C, 9 * NY, 128), state(4), state(9), state(9), state(), state(M),
        state(), state(), state(), state(), state(), state(), state(),
        vmem(NY, 2 * W), window(2 * NX), window(NZ), window(),
        window(), window(), window(), state(n_tm // (NX * NZ) - 1),
        window(NX + 1), window(NX + 1), window(NX + 1), state(2), state(2), state(n_tm // (NX * NZ) - 1),
        state(), vmem(M, 16, W), vmem(M, 16, W),
        pltpu.SemaphoreType.DMA((16,)), pltpu.SemaphoreType.DMA((24,)), pltpu.SemaphoreType.DMA((2,)),
    ]
    return pl.pallas_call(
        functools.partial(kernel, n_tm),
        out_shape=jax.ShapeDtypeStruct(args[0].shape, F32),
        in_specs=[pl.BlockSpec(memory_space=pltpu.HBM)] * 6,
        out_specs=pl.BlockSpec(memory_space=pltpu.HBM),
        scratch_shapes=scratch,
        compiler_params=pltpu.CompilerParams(
            collective_id=0, has_side_effects=True, vmem_limit_bytes=60 * 1024 * 1024
        ),
    )(*args)


def solution(mesh):
    placed = (
        P("tm", "space", None),
        P("space", None),
        P("space", None),
        P("space", None),
        P("space", None),
        P("space", None),
    )
    return jax.shard_map(
        functools.partial(body, mesh.shape["tm"]),
        mesh=mesh, in_specs=placed, out_specs=P("tm", "space", None), check_vma=False,
    )
```

```python
import functools

import jax
import jax.numpy as jnp
from jax import lax
from jax.experimental import pallas as pl
from jax.experimental.pallas import tpu as pltpu
from jax.sharding import PartitionSpec as P

M = 8
NX = 4
NZ = 8
C = 4
R = 4
T = (8, 128)
W = 128 * C
NY = 8 * R
MESH = pl.DeviceIdType.MESH
BF16 = jnp.bfloat16
F32 = jnp.float32


def tile(ref, lead, r, c):
    return ref[(*lead, pl.ds(8 * r, 8), pl.ds(128 * c, 128))]


def load_state(ref, *lead, columns=C):
    return [[tile(ref, lead, r, c) for r in range(R)] for c in range(columns)]


def store_state(ref, v, *lead):
    for c, column in enumerate(v):
        for r in range(R):
            ref[(*lead, pl.ds(8 * r, 8), pl.ds(128 * c, 128))] = column[r]


def load_win(ref, *lead):
    return load_state(ref, *lead, columns=1)[0]


def store_win(ref, v, *lead):
    store_state(ref, [v], *lead)


def add(a, b):
    if isinstance(a, list):
        return [add(x, y) for x, y in zip(a, b)]
    return a + b


def sub(a, b):
    if isinstance(a, list):
        return [sub(x, y) for x, y in zip(a, b)]
    return a - b


def iota(shape, dim):
    return lax.broadcasted_iota(jnp.int32, shape, dim)


def at_row(column, r, di):
    carry, index = divmod(r + di, R)
    x = column[index]
    return x if carry == 0 else pltpu.roll(x, (-carry) % 8, 0)


def beside(v, width):
    ext = {c: v[c] for c in range(C)}
    for j in range(1, width + 1):
        ext[-j] = [pltpu.roll(x, 1, 1) for x in v[C - j]]
        ext[C - 1 + j] = [pltpu.roll(x, 127, 1) for x in v[j - 1]]
    return ext


def advance(states, coef, first, count, source=None):
    exts = [beside(v, count) for v in states]
    for j in range(count):
        width = count - 1 - j
        news = [{} for _ in exts]
        for c in range(-width, C + width):
            for n in news:
                n[c] = []
            for r in range(R):
                k0, kl, kr, ku, kd = (tile(coef, (k,), r, c - first) for k in range(5))
                plus = None if source is None else tile(source, (), r, c)
                for n, e in zip(news, exts):
                    new = (k0 * e[c][r] + kl * e[c - 1][r]) + (kr * e[c + 1][r] + ku * at_row(e[c], r, -1))
                    new = new + kd * at_row(e[c], r, 1)
                    n[c].append(new if plus is None else new + plus)
        exts = news
    return [[e[c] for c in range(C)] for e in exts]


def relax(states, coef, source):
    return lax.fori_loop(0, M, lambda _, s: advance(s, coef, 0, 1, source), states)


def move(v, coef, times, count=2, unroll=1):
    def some(_, s):
        for _ in range(unroll):
            s = advance(s, coef, -1, count)
        return s

    return lax.fori_loop(0, times, some, [v])[0]


ONE = [(0, 0), (0, -1), (0, 1), (-1, 0), (1, 0)]


def sums(a, b):
    out = []
    for d in a:
        for e in b:
            f = (d[0] + e[0], d[1] + e[1])
            if f not in out:
                out.append(f)
    return out


TWO = sums(ONE, ONE)
FOUR = sums(TWO, TWO)


def along(v, dj):
    return v if dj == 0 else [pltpu.roll(x, (-dj) % 128, 1) for x in v]


def win_apply(v, coef, offsets):
    moved = {dj: along(v, dj) for dj in sorted({d[1] for d in offsets})}
    out = []
    for r in range(R):
        parts = [None] * 4
        for n, (di, dj) in enumerate(offsets):
            term = tile(coef, (n,), r, 0) * at_row(moved[dj], r, di)
            parts[n % 4] = term if parts[n % 4] is None else parts[n % 4] + term
        out.append((parts[0] + parts[1]) + (parts[2] + parts[3]))
    return out


def compose(out, a, a_offsets, b, b_offsets, out_offsets):
    seen = set()
    for dj in sorted({d[1] for d in a_offsets}):
        for n, e in enumerate(b_offsets):
            moved = along(load_win(b, n), dj)
            for m, d in enumerate(a_offsets):
                if d[1] != dj:
                    continue
                k = out_offsets.index((d[0] + e[0], d[1] + e[1]))
                for r in range(R):
                    term = tile(a, (m,), r, 0) * at_row(moved, r, d[0])
                    if k in seen:
                        term = term + tile(out, (k,), r, 0)
                    out[k, pl.ds(8 * r, 8), :] = term
                seen.add(k)


def permuted(x, matrix):
    high = x.astype(BF16)
    rest = x - high.astype(F32)
    mid = rest.astype(BF16)
    low = (rest - mid.astype(F32)).astype(BF16)
    count = x.shape[0]
    parts = jnp.concatenate([high, mid, low], axis=0)
    out = jnp.dot(parts, matrix, preferred_element_type=F32)
    return (out[:count] + out[count : 2 * count]) + out[2 * count :]


def selector(row_of_column):
    return jnp.where(iota((W, W), 0) == row_of_column, 1.0, 0.0).astype(BF16)


def inner_place(column):
    return 128 * lax.rem(column, C) + lax.div(column, C)


def merged(own, other, band):
    lane = iota(T, 1)
    low = band == 0
    out = []
    for a, b in zip(own, other):
        w0, w1 = jnp.where(low, a, b), jnp.where(low, b, a)
        out.append(jnp.where(lane < 64, pltpu.roll(w0, 96, 1), pltpu.roll(w1, 32, 1)))
    return out


def kernel(
    n_tm, cpoints, initial, diffusion, velocity_x, velocity_y, source, out,
    raw, perm_in, perm_win, perm_out, c1, c8, c64, src, init, cw1, cw2, cw4, cwide, rows, cpi, rel, prl, relm, dfc,
    u_own, u_sib, u_sum, up, term, mid, lag, w1s, w1, u1, pz, t2own, t2sib, t2m, t2, rown, rsib, rm, rr, rri, t2i,
    fbuf, outi, outb, send, recv, loc, round_sem,
):
    p = lax.axis_index("tm")
    s = lax.axis_index("space")
    x = lax.rem(p, NX)
    g = lax.div(p, NX)
    z = lax.rem(g, NZ)
    y = lax.div(g, NZ)
    n_y = n_tm // (NX * NZ)
    plane = NX * NZ
    other = 1 - s
    row0 = pl.multiple_of(16 * s, 16)
    band = pl.ds(row0, 16)
    base = 4 * s
    first_slab = p == 0

    def dev(tm, space):
        return {"tm": tm, "space": space}

    def cols(c):
        return pl.ds(pl.multiple_of(128 * c, 128), 128)

    near = [dev(p, other)]
    for d in (1, NX - 1):
        near.append(dev(NX * g + lax.rem(x + d, NX), s))
    for d in (1, NZ - 1):
        near.append(dev(plane * y + NX * lax.rem(z + d, NZ) + x, s))
    for d in (1, n_y - 1):
        near.append(dev(plane * lax.rem(y + d, n_y) + NX * z + x, s))

    def tell(sem):
        for to in near:
            pl.semaphore_signal(sem, inc=1, device_id=to, device_id_type=MESH)

    def hear(sem):
        pl.semaphore_wait(sem, len(near))

    barrier = pltpu.get_barrier_semaphore()
    tell(barrier)

    fields = (diffusion, velocity_x, velocity_y, source, initial)
    for k, f in enumerate(fields):
        pltpu.make_async_copy(f, raw.at[k, band, :], loc.at[0]).start()
    pltpu.make_async_copy(cpoints.at[pl.ds(base, 4)], raw.at[pl.ds(5, 4), band, :], loc.at[0]).start()

    hear(barrier)
    tell(round_sem.at[0])

    def remote(src_ref, dst_ref, to, send_idx, recv_idx):
        return pltpu.make_async_remote_copy(
            src_ref=src_ref, dst_ref=dst_ref, send_sem=send.at[send_idx], recv_sem=recv.at[recv_idx],
            device_id=to, device_id_type=MESH,
        )

    def whole(ref, idx):
        return remote(ref, ref, dev(p, other), idx, idx)

    for k, f in enumerate(fields):
        remote(f, raw.at[k, band, :], dev(p, other), 0, 0).start()
    remote(cpoints.at[pl.ds(4 * other, 4)], raw.at[pl.ds(5, 4), band, :], dev(p, other), 0, 0).start()
    sib = whole(raw.at[pl.ds(0, 9), band, :], 0)

    line = iota((1, W), 1)
    perm_in[...] = selector(C * lax.rem(line, 128) + lax.div(line, 128))
    for ss in range(2):
        begin = 128 * lax.div(line, 128) + (64 * ss + W - 32)
        perm_win[:, pl.ds(W * ss, W)] = selector(inner_place(lax.rem(begin + lax.rem(line, 128), W)))

    pltpu.make_async_copy(raw.at[pl.ds(0, 9), band, :], raw.at[pl.ds(0, 9), band, :], loc.at[0]).wait()
    sib.wait_recv()

    def inward(first, count, emit):
        moved = permuted(raw[pl.ds(first, count)].reshape(count * NY, W), perm_in[...])
        for c in range(C):
            rows[c, pl.ds(0, count * NY), :] = moved[:, 128 * c : 128 * (c + 1)]
        for k in range(count):
            emit(k, [[rows[c, pl.ds(NY * k + r, 8, stride=R), :] for r in range(R)] for c in range(C)])

    got = {}

    def keep(k, v):
        if k < 3:
            got[k] = v
        elif k == 3:
            store_state(src, v)
        elif k == 4:
            store_state(init, v)
        else:
            store_state(cpi, v, k - 5)

    inward(0, 9, keep)
    hear(round_sem.at[0])
    tell(round_sem.at[1])

    sub_row = iota(T, 0)
    for c in range(C):
        for r in range(R):
            d, vx, vy = (got[k][c][r] for k in range(3))
            k0 = 4.0 * d + (jnp.abs(vx) + jnp.abs(vy))
            kl = d + jnp.maximum(vx, 0.0)
            kr = d - jnp.minimum(vx, 0.0)
            ku = d + jnp.maximum(vy, 0.0)
            kd = d - jnp.minimum(vy, 0.0)
            if r == 0:
                ku = jnp.where(sub_row == 0, 0.0, ku)
            if r == R - 1:
                kd = jnp.where(sub_row == 7, 0.0, kd)
            here = (pl.ds(8 * r, 8), pl.ds(128 * c, 128))
            wide = (pl.ds(8 * r, 8), pl.ds(128 * (c + 1), 128))
            for ref, scale, at in ((c1, 1.0, here), (c8, 8.0, wide), (c64, 64.0, wide)):
                ref[(0, *at)] = 1.0 - scale * k0
                for k, val in enumerate((kl, kr, ku, kd)):
                    ref[(k + 1, *at)] = scale * val

    for ref in (c8, c64):
        for k in range(5):
            for r in range(R):
                ref[k, pl.ds(8 * r, 8), pl.ds(0, 128)] = pltpu.roll(tile(ref, (k,), r, C), 1, 1)
                ref[k, pl.ds(8 * r, 8), pl.ds(128 * (C + 1), 128)] = pltpu.roll(tile(ref, (k,), r, 1), 127, 1)

    def relax_own(extra):
        once = relax([load_state(cpi, k) for k in range(4)] + extra, c1, src)
        for k in range(4):
            store_state(rel, once[k], base + 1 + k)
        twice = relax(once, c1, src)
        for k in range(4):
            store_state(prl, twice[k], base + 1 + k)
        if extra:
            store_state(mid, twice[4])

    opens = jnp.logical_and(first_slab, s == 0)

    @pl.when(opens)
    def _():
        relax_own([load_state(init)])

    @pl.when(jnp.logical_not(opens))
    def _():
        relax_own([])
        mid[...] = jnp.zeros_like(mid)

    hear(round_sem.at[1])
    tell(round_sem.at[2])

    head = sub(load_state(mid), load_state(rel, base + 1))

    def defect(k):
        return sub(load_state(prl, base + k - 1), load_state(rel, base + k))

    head, late = advance([head, defect(4)], c8, -1, 1)
    head = add(head, defect(2))
    late = add(late, load_state(prl, base + 4))
    (head,) = advance([head], c8, -1, 1)
    store_state(fbuf, add(head, defect(3)))
    store_state(term, late)

    @pl.when(s == 0)
    def _():
        v = move(load_state(fbuf), c8, 1)
        v = move(add(v, load_state(term)), c8, 5)
        store_state(u_own, v)
        store_state(term, advance([v], c64, -1, 1)[0])

    @pl.when(s == 1)
    def _():
        a, b = lax.fori_loop(
            0, 4, lambda _, v: advance(v, c8, -1, 2), [load_state(fbuf), load_state(term)]
        )
        store_state(u_own, a)
        b = move(b, c8, 3)
        store_state(term, add(advance([a], c64, -1, 1)[0], b))

    w1s[...] = permuted(term[...], perm_win[...])
    for d in (2, 1, 3, 0):
        for flip in (0, 1):
            if d == 0 and flip == 0:
                continue
            xx, ss = lax.rem(x + d, NX), lax.rem(s + flip, 2)
            remote(w1s.at[:, cols(NX * ss + xx)], w1.at[2 * x + s], dev(NX * g + xx, ss), 2, 2).start()
    to_x = whole(w1.at[pl.ds(0, 2 * NX - 1)], 2)
    own = cols(NX * s + x)
    store_win(w1, [w1s[pl.ds(8 * r, 8), own] for r in range(R)], 2 * x + s)

    half = pl.ds(base + 1, 4)
    remote(u_own, u_sib, dev(p, other), 3, 3).start()
    remote(rel.at[half], rel.at[half], dev(p, other), 3, 3).start()
    remote(prl.at[half], prl.at[half], dev(p, other), 3, 3).start()
    shared = whole(rel, 3)

    hear(round_sem.at[2])

    @pl.when(p < n_tm - 1)
    def _():
        for ss in range(2):
            remote(cpoints.at[pl.ds(6, 2)], raw.at[pl.ds(9, 2), band, :], dev(p + 1, ss), 1, 1).start()

    ahead = whole(raw.at[pl.ds(9, 2)], 1)

    cwide[...] = permuted(
        c64[:, :, pl.ds(128, W)].reshape(5 * NY, W), perm_win[:, pl.ds(pl.multiple_of(W * s, W), W)]
    )
    for k in range(5):
        cw1[k] = cwide[pl.ds(NY * k, NY), cols(x)]
    compose(cw2, cw1, ONE, cw1, ONE, TWO)
    compose(cw4, cw2, TWO, cw2, TWO, FOUR)

    to_x.wait_recv()

    def group_term(i):
        return add(load_win(w1, 2 * i), load_win(w1, 2 * i + 1))

    a = add(win_apply(group_term(0), cw1, ONE), group_term(1))
    b = add(win_apply(group_term(2), cw1, ONE), group_term(3))
    store_win(u1, add(win_apply(a, cw2, TWO), b), z)

    for d in (4, 3, 5, 2, 6, 1, 7):
        zz = lax.rem(z + d, NZ)
        remote(u1.at[z], u1.at[z], dev(plane * y + NX * zz + x, s), 4, 16 + z).start()
    to_z = whole(u1.at[pl.ds(0, NZ - 1)], 4)

    perm_out[...] = selector(inner_place(line))
    shared.wait_recv()
    store_state(u_sum, add(load_state(u_own), load_state(u_sib)))
    to_up = remote(u_sum, up, dev(p + 1, s), 5, 5)

    @pl.when(p < n_tm - 1)
    def _():
        to_up.start()

    @pl.when(p > 0)
    def _():
        ahead.wait_recv()
        inward(9, 2, lambda k, v: store_state(cpi, v, k))

    @pl.when(first_slab)
    def _():
        up[...] = jnp.zeros_like(up)
        for k in range(2):
            store_state(cpi, load_state(init), k)

    v = relax([load_state(cpi, 0), load_state(cpi, 1)], c1, src)
    store_state(relm, v[0])
    store_state(rel, v[1], 0)

    @pl.when(first_slab)
    def _():
        store_state(relm, load_state(init))

    v = relax([load_state(relm), load_state(rel, 0)], c1, src)
    store_state(dfc, sub(v[0], load_state(rel, 0)), 0)
    store_state(prl, v[1], 0)

    def climb(k, v):
        d = sub(load_state(prl, k - 1), load_state(rel, k))
        store_state(dfc, d, k)
        return add(advance([v], c8, -1, 1)[0], d)

    v = lax.fori_loop(1, M, climb, load_state(dfc, 0))

    store_state(mid, v)

    pz[...] = jnp.zeros_like(pz)

    @pl.when(z != 0)
    def _():
        remote(u1.at[0], u1.at[0], dev(p, other), 4, 16).wait_recv()

    def ascend(zz, acc):
        @pl.when(z == zz)
        def _():
            store_win(pz, acc)

        @pl.when(z != zz)
        def _():
            remote(u1.at[zz], u1.at[zz], dev(p, other), 4, 16 + zz).wait_recv()

        return add(win_apply(acc, cw4, FOUR), load_win(u1, zz))

    store_win(t2own, lax.fori_loop(1, NZ, ascend, load_win(u1, 0)))
    swap_t = remote(t2own, t2sib, dev(p, other), 7, 7)
    swap_t.start()

    acc = load_win(pz)
    store_win(rown, acc, 0)
    for i in range(NX):
        acc = add(win_apply(acc, cw1, ONE), group_term(i))
        store_win(rown, acc, i + 1)
    swap_r = remote(rown, rsib, dev(p, other), 8, 8)
    swap_r.start()

    swap_t.wait_recv()
    store_win(t2m, merged(load_win(t2own), load_win(t2sib), s))
    for yy in range(1, n_y):
        @pl.when(yy > y)
        def _():
            for xx in range(NX):
                remote(
                    t2m, t2.at[y, :, cols(x)], dev(plane * yy + NX * z + xx, s), 8 + yy, 10 + y
                ).start()

    swap_r.wait_recv()
    for i in range(NX + 1):
        store_win(rm, merged(load_win(rown, i), load_win(rsib, i), s), i)
    to_r = []
    for i in range(NX):
        there = NX * g + 2 + i
        copy = remote(rm.at[pl.ds(i, 2)], rr.at[:, :, cols(x)], dev(there, s), 12 + i, 9)
        go = x != i + 2 if i < 2 else there < n_tm
        to_r.append((go, copy))

        @pl.when(go)
        def _():
            copy.start()

        if i < 2:
            @pl.when(x == i + 2)
            def _():
                for j in range(2):
                    rr[j, :, cols(x)] = rm[i + j]

    @pl.when(p > 0)
    def _():
        to_up.wait_recv()

    store_state(mid, add(load_state(mid), load_state(up)))
    to_lag = remote(mid, lag, dev(p + 1, s), 6, 6)

    @pl.when(p < n_tm - 1)
    def _():
        to_lag.start()

    @pl.when(p < 2)
    def _():
        rr[...] = jnp.zeros_like(rr)

    @pl.when(first_slab)
    def _():
        lag[...] = jnp.zeros_like(lag)

    @pl.when(x >= 2)
    def _():
        whole(rr.at[:, :, pl.ds(0, W - 128)], 9).wait_recv()

    @pl.when(jnp.logical_and(x < 2, g > 0))
    def _():
        whole(rr, 9).wait_recv()

    rri[...] = permuted(rr[...].reshape(2 * NY, W), perm_in[...]).reshape(2, NY, W)

    q = jnp.maximum(p - 2, 0)
    n = lax.rem(q, plane)
    yq = lax.div(q, plane)
    fbuf[...] = jnp.zeros_like(fbuf)
    for yy in range(n_y - 1):
        @pl.when(yy < y)
        def _():
            whole(t2.at[yy], 10 + yy).wait_recv()

    t2i[...] = permuted(t2[...].reshape((n_y - 1) * NY, W), perm_in[...]).reshape(n_y - 1, NY, W)
    for yy in range(n_y - 1):
        @pl.when(yy < yq)
        def _():
            f = load_state(t2i, yy)
            if yy > 0:
                f = add(move(load_state(fbuf), c64, plane // 8, 2, 4), f)
            store_state(fbuf, f)

    n = jnp.where(yq > 0, n, 0)
    f = move(load_state(fbuf), c64, lax.div(n, 2))
    f = move(f, c64, lax.rem(n, 2), 1)
    e = add(f, load_state(rri, 0))
    (f,) = advance([f], c64, -1, 1)
    last = add(add(f, load_state(rri, 1)), load_state(mid))

    def emit(k, value):
        for c in range(C):
            for r in range(R):
                rows[c, pl.ds(r, 8, stride=R), :] = value[c][r]
        for c in range(C):
            for t in range(2):
                outi[k, pl.ds(8 * t, 8), pl.ds(128 * c, 128)] = rows[c, pl.ds(pl.multiple_of(row0 + 8 * t, 8), 8), :]

    emit(M - 1, add(last, load_state(rel, M - 1)))

    def errors(k, v):
        v = add(advance([v], c8, -1, 1)[0], load_state(dfc, k))
        emit(k, add(v, load_state(rel, k)))
        return v

    @pl.when(p > 0)
    def _():
        to_lag.wait_recv()

    lax.fori_loop(0, M - 1, errors, add(load_state(lag), e))
    outb[...] = permuted(outi[...].reshape(M * 16, W), perm_out[...]).reshape(M, 16, W)
    done = pltpu.make_async_copy(outb, out, loc.at[1])
    done.start()

    sib.wait_send()

    @pl.when(p < n_tm - 1)
    def _():
        ahead.wait_send()
        to_up.wait_send()
        to_lag.wait_send()

    for copy in (to_x, shared, to_z, swap_t, swap_r):
        copy.wait_send()
    for yy in range(1, n_y):
        @pl.when(yy > y)
        def _():
            whole(t2.at[0], 8 + yy).wait_send()

    for go, copy in to_r:
        @pl.when(go)
        def _():
            copy.wait_send()

    done.wait()


def body(n_tm, *args):
    def vmem(*shape, dtype=F32):
        return pltpu.VMEM(shape, dtype)

    def state(*lead):
        return vmem(*lead, NY, W)

    def window(*lead):
        return vmem(*lead, NY, 128)

    square = vmem(W, W, dtype=BF16)
    scratch = [
        state(11), square, vmem(W, 2 * W, dtype=BF16), square,
        state(5), vmem(5, NY, W + 256), vmem(5, NY, W + 256), state(), state(),
        window(len(ONE)), window(len(TWO)), window(len(FOUR)), vmem(5 * NY, W),
        vmem(C, 9 * NY, 128), state(4), state(9), state(9), state(), state(M),
        state(), state(), state(), state(), state(), state(), state(),
        vmem(NY, 2 * W), window(2 * NX), window(NZ), window(),
        window(), window(), window(), state(n_tm // (NX * NZ) - 1),
        window(NX + 1), window(NX + 1), window(NX + 1), state(2), state(2), state(n_tm // (NX * NZ) - 1),
        state(), vmem(M, 16, W), vmem(M, 16, W),
        pltpu.SemaphoreType.DMA((16,)), pltpu.SemaphoreType.DMA((24,)), pltpu.SemaphoreType.DMA((2,)),
        pltpu.SemaphoreType.REGULAR((3,)),
    ]
    return pl.pallas_call(
        functools.partial(kernel, n_tm),
        out_shape=jax.ShapeDtypeStruct(args[0].shape, F32),
        in_specs=[pl.BlockSpec(memory_space=pltpu.HBM)] * 6,
        out_specs=pl.BlockSpec(memory_space=pltpu.HBM),
        scratch_shapes=scratch,
        compiler_params=pltpu.CompilerParams(
            collective_id=0, has_side_effects=True, vmem_limit_bytes=60 * 1024 * 1024
        ),
    )(*args)


def solution(mesh):
    placed = (
        P("tm", "space", None),
        P("space", None),
        P("space", None),
        P("space", None),
        P("space", None),
        P("space", None),
    )
    return jax.shard_map(
        functools.partial(body, mesh.shape["tm"]),
        mesh=mesh, in_specs=placed, out_specs=P("tm", "space", None), check_vma=False,
    )
```

```python
import functools

import jax
import jax.numpy as jnp
from jax import lax
from jax.experimental import pallas as pl
from jax.experimental.pallas import tpu as pltpu
from jax.sharding import PartitionSpec as P

M = 8
NX = 4
NZ = 8
C = 4
R = 4
T = (8, 128)
W = 128 * C
NY = 8 * R
MESH = pl.DeviceIdType.MESH
BF16 = jnp.bfloat16
F32 = jnp.float32


def tile(ref, lead, r, c):
    return ref[(*lead, pl.ds(8 * r, 8), pl.ds(128 * c, 128))]


def load_state(ref, *lead, columns=C):
    return [[tile(ref, lead, r, c) for r in range(R)] for c in range(columns)]


def store_state(ref, v, *lead):
    for c, column in enumerate(v):
        for r in range(R):
            ref[(*lead, pl.ds(8 * r, 8), pl.ds(128 * c, 128))] = column[r]


def load_win(ref, *lead):
    return load_state(ref, *lead, columns=1)[0]


def store_win(ref, v, *lead):
    store_state(ref, [v], *lead)


def add(a, b):
    if isinstance(a, list):
        return [add(x, y) for x, y in zip(a, b)]
    return a + b


def sub(a, b):
    if isinstance(a, list):
        return [sub(x, y) for x, y in zip(a, b)]
    return a - b


def iota(shape, dim):
    return lax.broadcasted_iota(jnp.int32, shape, dim)


def at_row(column, r, di):
    carry, index = divmod(r + di, R)
    x = column[index]
    return x if carry == 0 else pltpu.roll(x, (-carry) % 8, 0)


def beside(v, width):
    ext = {c: v[c] for c in range(C)}
    for j in range(1, width + 1):
        ext[-j] = [pltpu.roll(x, 1, 1) for x in v[C - j]]
        ext[C - 1 + j] = [pltpu.roll(x, 127, 1) for x in v[j - 1]]
    return ext


def advance(states, coef, first, count, source=None):
    exts = [beside(v, count) for v in states]
    for j in range(count):
        width = count - 1 - j
        news = [{} for _ in exts]
        for c in range(-width, C + width):
            for n in news:
                n[c] = []
            for r in range(R):
                k0, kl, kr, ku, kd = (tile(coef, (k,), r, c - first) for k in range(5))
                plus = None if source is None else tile(source, (), r, c)
                for n, e in zip(news, exts):
                    new = (k0 * e[c][r] + kl * e[c - 1][r]) + (kr * e[c + 1][r] + ku * at_row(e[c], r, -1))
                    new = new + kd * at_row(e[c], r, 1)
                    n[c].append(new if plus is None else new + plus)
        exts = news
    return [[e[c] for c in range(C)] for e in exts]


def relax(states, coef, source):
    return lax.fori_loop(0, M, lambda _, s: advance(s, coef, 0, 1, source), states)


def move(v, coef, times, count=2, unroll=1):
    def some(_, s):
        for _ in range(unroll):
            s = advance(s, coef, -1, count)
        return s

    return lax.fori_loop(0, times, some, [v])[0]


ONE = [(0, 0), (0, -1), (0, 1), (-1, 0), (1, 0)]


def sums(a, b):
    out = []
    for d in a:
        for e in b:
            f = (d[0] + e[0], d[1] + e[1])
            if f not in out:
                out.append(f)
    return out


TWO = sums(ONE, ONE)
FOUR = sums(TWO, TWO)


def along(v, dj):
    return v if dj == 0 else [pltpu.roll(x, (-dj) % 128, 1) for x in v]


def win_apply(v, coef, offsets):
    moved = {dj: along(v, dj) for dj in sorted({d[1] for d in offsets})}
    out = []
    for r in range(R):
        parts = [None] * 4
        for n, (di, dj) in enumerate(offsets):
            term = tile(coef, (n,), r, 0) * at_row(moved[dj], r, di)
            parts[n % 4] = term if parts[n % 4] is None else parts[n % 4] + term
        out.append((parts[0] + parts[1]) + (parts[2] + parts[3]))
    return out


def compose(out, a, a_offsets, b, b_offsets, out_offsets):
    seen = set()
    for dj in sorted({d[1] for d in a_offsets}):
        for n, e in enumerate(b_offsets):
            moved = along(load_win(b, n), dj)
            for m, d in enumerate(a_offsets):
                if d[1] != dj:
                    continue
                k = out_offsets.index((d[0] + e[0], d[1] + e[1]))
                for r in range(R):
                    term = tile(a, (m,), r, 0) * at_row(moved, r, d[0])
                    if k in seen:
                        term = term + tile(out, (k,), r, 0)
                    out[k, pl.ds(8 * r, 8), :] = term
                seen.add(k)


def permuted(x, matrix):
    high = x.astype(BF16)
    rest = x - high.astype(F32)
    mid = rest.astype(BF16)
    low = (rest - mid.astype(F32)).astype(BF16)
    count = x.shape[0]
    parts = jnp.concatenate([high, mid, low], axis=0)
    out = jnp.dot(parts, matrix, preferred_element_type=F32)
    return (out[:count] + out[count : 2 * count]) + out[2 * count :]


def selector(row_of_column):
    return jnp.where(iota((W, W), 0) == row_of_column, 1.0, 0.0).astype(BF16)


def inner_place(column):
    return 128 * lax.rem(column, C) + lax.div(column, C)


def merged(own, other, band):
    lane = iota(T, 1)
    low = band == 0
    out = []
    for a, b in zip(own, other):
        out.append(jnp.where(low == (lane < 64), a, b))
    return out


def kernel(
    n_tm, cpoints, initial, diffusion, velocity_x, velocity_y, source, out,
    raw, perm_in, perm_win, perm_out, c1, c8, c64, src, init, cw1, cw2, cw4, cwide, rows, cpi, rel, prl, relm, dfc,
    u_own, u_sib, u_sum, up, term, mid, lag, w1s, w1, u1, pz, t2own, t2sib, t2m, t2, rown, rsib, rm, rr, rri, t2i,
    fbuf, outi, outb, send, recv, loc, round_sem,
):
    p = lax.axis_index("tm")
    s = lax.axis_index("space")
    x = lax.rem(p, NX)
    g = lax.div(p, NX)
    z = lax.rem(g, NZ)
    y = lax.div(g, NZ)
    n_y = n_tm // (NX * NZ)
    plane = NX * NZ
    other = 1 - s
    row0 = pl.multiple_of(16 * s, 16)
    band = pl.ds(row0, 16)
    base = 4 * s
    first_slab = p == 0

    def dev(tm, space):
        return {"tm": tm, "space": space}

    def cols(c):
        return pl.ds(pl.multiple_of(128 * c, 128), 128)

    near = [dev(p, other)]
    for d in (1, NX - 1):
        near.append(dev(NX * g + lax.rem(x + d, NX), s))
    for d in (1, NZ - 1):
        near.append(dev(plane * y + NX * lax.rem(z + d, NZ) + x, s))
    for d in (1, n_y - 1):
        near.append(dev(plane * lax.rem(y + d, n_y) + NX * z + x, s))

    def tell(sem):
        for to in near:
            pl.semaphore_signal(sem, inc=1, device_id=to, device_id_type=MESH)

    def hear(sem):
        pl.semaphore_wait(sem, len(near))

    barrier = pltpu.get_barrier_semaphore()
    tell(barrier)

    fields = (diffusion, velocity_x, velocity_y, source, initial)
    for k, f in enumerate(fields):
        pltpu.make_async_copy(f, raw.at[k, band, :], loc.at[0]).start()
    pltpu.make_async_copy(cpoints.at[pl.ds(base, 4)], raw.at[pl.ds(5, 4), band, :], loc.at[0]).start()

    hear(barrier)
    tell(round_sem.at[0])

    def remote(src_ref, dst_ref, to, send_idx, recv_idx):
        return pltpu.make_async_remote_copy(
            src_ref=src_ref, dst_ref=dst_ref, send_sem=send.at[send_idx], recv_sem=recv.at[recv_idx],
            device_id=to, device_id_type=MESH,
        )

    def whole(ref, idx):
        return remote(ref, ref, dev(p, other), idx, idx)

    for k, f in enumerate(fields):
        remote(f, raw.at[k, band, :], dev(p, other), 0, 0).start()
    remote(cpoints.at[pl.ds(4 * other, 4)], raw.at[pl.ds(5, 4), band, :], dev(p, other), 0, 0).start()
    sib = whole(raw.at[pl.ds(0, 9), band, :], 0)

    line = iota((1, W), 1)
    perm_in[...] = selector(C * lax.rem(line, 128) + lax.div(line, 128))
    for ss in range(2):
        begin = 128 * lax.div(line, 128) + (64 * ss + W - 32)
        turned = lax.rem(lax.rem(line, 128) + 32 + 64 * ss, 128)
        perm_win[:, pl.ds(W * ss, W)] = selector(inner_place(lax.rem(begin + turned, W)))

    pltpu.make_async_copy(raw.at[pl.ds(0, 9), band, :], raw.at[pl.ds(0, 9), band, :], loc.at[0]).wait()
    sib.wait_recv()

    def inward(first, count, emit):
        moved = permuted(raw[pl.ds(first, count)].reshape(count * NY, W), perm_in[...])
        for c in range(C):
            rows[c, pl.ds(0, count * NY), :] = moved[:, 128 * c : 128 * (c + 1)]
        for k in range(count):
            emit(k, [[rows[c, pl.ds(NY * k + r, 8, stride=R), :] for r in range(R)] for c in range(C)])

    got = {}

    def keep(k, v):
        if k < 3:
            got[k] = v
        elif k == 3:
            store_state(src, v)
        elif k == 4:
            store_state(init, v)
        else:
            store_state(cpi, v, k - 5)

    inward(0, 9, keep)
    hear(round_sem.at[0])
    tell(round_sem.at[1])

    sub_row = iota(T, 0)
    for c in range(C):
        for r in range(R):
            d, vx, vy = (got[k][c][r] for k in range(3))
            k0 = 4.0 * d + (jnp.abs(vx) + jnp.abs(vy))
            kl = d + jnp.maximum(vx, 0.0)
            kr = d - jnp.minimum(vx, 0.0)
            ku = d + jnp.maximum(vy, 0.0)
            kd = d - jnp.minimum(vy, 0.0)
            if r == 0:
                ku = jnp.where(sub_row == 0, 0.0, ku)
            if r == R - 1:
                kd = jnp.where(sub_row == 7, 0.0, kd)
            here = (pl.ds(8 * r, 8), pl.ds(128 * c, 128))
            wide = (pl.ds(8 * r, 8), pl.ds(128 * (c + 1), 128))
            for ref, scale, at in ((c1, 1.0, here), (c8, 8.0, wide), (c64, 64.0, wide)):
                ref[(0, *at)] = 1.0 - scale * k0
                for k, val in enumerate((kl, kr, ku, kd)):
                    ref[(k + 1, *at)] = scale * val

    for ref in (c8, c64):
        for k in range(5):
            for r in range(R):
                ref[k, pl.ds(8 * r, 8), pl.ds(0, 128)] = pltpu.roll(tile(ref, (k,), r, C), 1, 1)
                ref[k, pl.ds(8 * r, 8), pl.ds(128 * (C + 1), 128)] = pltpu.roll(tile(ref, (k,), r, 1), 127, 1)

    def relax_own(extra):
        once = relax([load_state(cpi, k) for k in range(4)] + extra, c1, src)
        for k in range(4):
            store_state(rel, once[k], base + 1 + k)
        twice = relax(once, c1, src)
        for k in range(4):
            store_state(prl, twice[k], base + 1 + k)
        if extra:
            store_state(mid, twice[4])

    opens = jnp.logical_and(first_slab, s == 0)

    @pl.when(opens)
    def _():
        relax_own([load_state(init)])

    @pl.when(jnp.logical_not(opens))
    def _():
        relax_own([])
        mid[...] = jnp.zeros_like(mid)

    hear(round_sem.at[1])
    tell(round_sem.at[2])

    head = sub(load_state(mid), load_state(rel, base + 1))

    def defect(k):
        return sub(load_state(prl, base + k - 1), load_state(rel, base + k))

    head, late = advance([head, defect(4)], c8, -1, 1)
    head = add(head, defect(2))
    late = add(late, load_state(prl, base + 4))
    (head,) = advance([head], c8, -1, 1)
    store_state(fbuf, add(head, defect(3)))
    store_state(term, late)

    @pl.when(s == 0)
    def _():
        v = move(load_state(fbuf), c8, 1)
        v = move(add(v, load_state(term)), c8, 5)
        store_state(u_own, v)
        store_state(term, advance([v], c64, -1, 1)[0])

    @pl.when(s == 1)
    def _():
        a, b = lax.fori_loop(
            0, 4, lambda _, v: advance(v, c8, -1, 2), [load_state(fbuf), load_state(term)]
        )
        store_state(u_own, a)
        b = move(b, c8, 3)
        store_state(term, add(advance([a], c64, -1, 1)[0], b))

    w1s[...] = permuted(term[...], perm_win[...])
    for d in (2, 1, 3, 0):
        for flip in (0, 1):
            if d == 0 and flip == 0:
                continue
            xx, ss = lax.rem(x + d, NX), lax.rem(s + flip, 2)
            remote(w1s.at[:, cols(NX * ss + xx)], w1.at[2 * x + s], dev(NX * g + xx, ss), 2, 2).start()
    to_x = whole(w1.at[pl.ds(0, 2 * NX - 1)], 2)
    own = cols(NX * s + x)
    store_win(w1, [w1s[pl.ds(8 * r, 8), own] for r in range(R)], 2 * x + s)

    half = pl.ds(base + 1, 4)
    remote(u_own, u_sib, dev(p, other), 3, 3).start()
    remote(rel.at[half], rel.at[half], dev(p, other), 3, 3).start()
    remote(prl.at[half], prl.at[half], dev(p, other), 3, 3).start()
    shared = whole(rel, 3)

    hear(round_sem.at[2])

    @pl.when(p < n_tm - 1)
    def _():
        for ss in range(2):
            remote(cpoints.at[pl.ds(6, 2)], raw.at[pl.ds(9, 2), band, :], dev(p + 1, ss), 1, 1).start()

    ahead = whole(raw.at[pl.ds(9, 2)], 1)

    cwide[...] = permuted(
        c64[:, :, pl.ds(128, W)].reshape(5 * NY, W), perm_win[:, pl.ds(pl.multiple_of(W * s, W), W)]
    )
    for k in range(5):
        cw1[k] = cwide[pl.ds(NY * k, NY), cols(x)]
    compose(cw2, cw1, ONE, cw1, ONE, TWO)
    compose(cw4, cw2, TWO, cw2, TWO, FOUR)

    to_x.wait_recv()

    def group_term(i):
        return add(load_win(w1, 2 * i), load_win(w1, 2 * i + 1))

    a = add(win_apply(group_term(0), cw1, ONE), group_term(1))
    b = add(win_apply(group_term(2), cw1, ONE), group_term(3))
    store_win(u1, add(win_apply(a, cw2, TWO), b), z)

    for d in (4, 3, 5, 2, 6, 1, 7):
        zz = lax.rem(z + d, NZ)
        remote(u1.at[z], u1.at[z], dev(plane * y + NX * zz + x, s), 4, 16 + z).start()
    to_z = whole(u1.at[pl.ds(0, NZ - 1)], 4)

    perm_out[...] = selector(inner_place(line))
    shared.wait_recv()
    store_state(u_sum, add(load_state(u_own), load_state(u_sib)))
    to_up = remote(u_sum, up, dev(p + 1, s), 5, 5)

    @pl.when(p < n_tm - 1)
    def _():
        to_up.start()

    @pl.when(p > 0)
    def _():
        ahead.wait_recv()
        inward(9, 2, lambda k, v: store_state(cpi, v, k))

    @pl.when(first_slab)
    def _():
        up[...] = jnp.zeros_like(up)
        for k in range(2):
            store_state(cpi, load_state(init), k)

    v = relax([load_state(cpi, 0), load_state(cpi, 1)], c1, src)
    store_state(relm, v[0])
    store_state(rel, v[1], 0)

    @pl.when(first_slab)
    def _():
        store_state(relm, load_state(init))

    v = relax([load_state(relm), load_state(rel, 0)], c1, src)
    store_state(dfc, sub(v[0], load_state(rel, 0)), 0)
    store_state(prl, v[1], 0)

    def climb(k, v):
        d = sub(load_state(prl, k - 1), load_state(rel, k))
        store_state(dfc, d, k)
        return add(advance([v], c8, -1, 1)[0], d)

    v = lax.fori_loop(1, M, climb, load_state(dfc, 0))

    store_state(mid, v)

    pz[...] = jnp.zeros_like(pz)

    @pl.when(z != 0)
    def _():
        remote(u1.at[0], u1.at[0], dev(p, other), 4, 16).wait_recv()

    def ascend(zz, acc):
        @pl.when(z == zz)
        def _():
            store_win(pz, acc)

        @pl.when(z != zz)
        def _():
            remote(u1.at[zz], u1.at[zz], dev(p, other), 4, 16 + zz).wait_recv()

        return add(win_apply(acc, cw4, FOUR), load_win(u1, zz))

    store_win(t2own, lax.fori_loop(1, NZ, ascend, load_win(u1, 0)))
    swap_t = remote(t2own, t2sib, dev(p, other), 7, 7)
    swap_t.start()

    acc = load_win(pz)
    store_win(rown, acc, 0)
    for i in range(NX):
        acc = add(win_apply(acc, cw1, ONE), group_term(i))
        store_win(rown, acc, i + 1)
    swap_r = remote(rown, rsib, dev(p, other), 8, 8)
    swap_r.start()

    swap_t.wait_recv()
    store_win(t2m, merged(load_win(t2own), load_win(t2sib), s))
    for yy in range(n_y - 1, 0, -1):
        @pl.when(yy > y)
        def _():
            for xx in range(NX):
                remote(
                    t2m, t2.at[y, :, cols(x)], dev(plane * yy + NX * z + xx, s), 8 + yy, 10 + y
                ).start()

    swap_r.wait_recv()
    for i in range(NX + 1):
        store_win(rm, merged(load_win(rown, i), load_win(rsib, i), s), i)
    to_r = []
    for i in range(NX):
        there = NX * g + 2 + i
        copy = remote(rm.at[pl.ds(i, 2)], rr.at[:, :, cols(x)], dev(there, s), 12 + i, 9)
        go = x != i + 2 if i < 2 else there < n_tm
        to_r.append((go, copy))

        @pl.when(go)
        def _():
            copy.start()

        if i < 2:
            @pl.when(x == i + 2)
            def _():
                for j in range(2):
                    rr[j, :, cols(x)] = rm[i + j]

    @pl.when(p > 0)
    def _():
        to_up.wait_recv()

    store_state(mid, add(load_state(mid), load_state(up)))
    to_lag = remote(mid, lag, dev(p + 1, s), 6, 6)

    @pl.when(p < n_tm - 1)
    def _():
        to_lag.start()

    @pl.when(p < 2)
    def _():
        rr[...] = jnp.zeros_like(rr)

    @pl.when(first_slab)
    def _():
        lag[...] = jnp.zeros_like(lag)

    q = jnp.maximum(p - 2, 0)
    n = lax.rem(q, plane)
    yq = lax.div(q, plane)
    fbuf[...] = jnp.zeros_like(fbuf)
    for yy in range(n_y - 1):
        @pl.when(yy < yq)
        def _():
            if yy > 0:
                v = move(load_state(fbuf), c64, (plane - 4) // 4, 2, 2)
            whole(t2.at[yy], 10 + yy).wait_recv()
            t2i[...] = permuted(t2[yy], perm_in[...])
            if yy > 0:
                for _ in range(2):
                    (v,) = advance([v], c64, -1, 2)
            f = load_state(t2i)
            store_state(fbuf, add(v, f) if yy > 0 else f)

    n = jnp.where(yq > 0, n, 0)
    f = move(load_state(fbuf), c64, lax.div(n, 2))
    f = move(f, c64, lax.rem(n, 2), 1)

    @pl.when(x >= 2)
    def _():
        whole(rr.at[:, :, pl.ds(0, W - 128)], 9).wait_recv()

    @pl.when(jnp.logical_and(x < 2, g > 0))
    def _():
        whole(rr, 9).wait_recv()

    @pl.when(p > 0)
    def _():
        to_lag.wait_recv()

    rri[...] = permuted(rr[...].reshape(2 * NY, W), perm_in[...]).reshape(2, NY, W)

    e = add(f, load_state(rri, 0))
    (f,) = advance([f], c64, -1, 1)
    last = add(add(f, load_state(rri, 1)), load_state(mid))

    def emit(k, value):
        for c in range(C):
            for r in range(R):
                rows[c, pl.ds(r, 8, stride=R), :] = value[c][r]
        for c in range(C):
            for t in range(2):
                outi[k, pl.ds(8 * t, 8), pl.ds(128 * c, 128)] = rows[c, pl.ds(pl.multiple_of(row0 + 8 * t, 8), 8), :]

    emit(M - 1, add(last, load_state(rel, M - 1)))

    def errors(k, v):
        v = add(advance([v], c8, -1, 1)[0], load_state(dfc, k))
        emit(k, add(v, load_state(rel, k)))
        return v

    lax.fori_loop(0, M - 1, errors, add(load_state(lag), e))
    outb[...] = permuted(outi[...].reshape(M * 16, W), perm_out[...]).reshape(M, 16, W)
    done = pltpu.make_async_copy(outb, out, loc.at[1])
    done.start()

    for yy in range(n_y - 1):
        @pl.when(jnp.logical_and(yy >= yq, yy < y))
        def _():
            whole(t2.at[yy], 10 + yy).wait_recv()

    sib.wait_send()

    @pl.when(p < n_tm - 1)
    def _():
        ahead.wait_send()
        to_up.wait_send()
        to_lag.wait_send()

    for copy in (to_x, shared, to_z, swap_t, swap_r):
        copy.wait_send()
    for yy in range(1, n_y):
        @pl.when(yy > y)
        def _():
            whole(t2.at[0], 8 + yy).wait_send()

    for go, copy in to_r:
        @pl.when(go)
        def _():
            copy.wait_send()

    done.wait()


def body(n_tm, *args):
    def vmem(*shape, dtype=F32):
        return pltpu.VMEM(shape, dtype)

    def state(*lead):
        return vmem(*lead, NY, W)

    def window(*lead):
        return vmem(*lead, NY, 128)

    square = vmem(W, W, dtype=BF16)
    scratch = [
        state(11), square, vmem(W, 2 * W, dtype=BF16), square,
        state(5), vmem(5, NY, W + 256), vmem(5, NY, W + 256), state(), state(),
        window(len(ONE)), window(len(TWO)), window(len(FOUR)), vmem(5 * NY, W),
        vmem(C, 9 * NY, 128), state(4), state(9), state(9), state(), state(M),
        state(), state(), state(), state(), state(), state(), state(),
        vmem(NY, 2 * W), window(2 * NX), window(NZ), window(),
        window(), window(), window(), state(n_tm // (NX * NZ) - 1),
        window(NX + 1), window(NX + 1), window(NX + 1), state(2), state(2), state(),
        state(), vmem(M, 16, W), vmem(M, 16, W),
        pltpu.SemaphoreType.DMA((16,)), pltpu.SemaphoreType.DMA((24,)), pltpu.SemaphoreType.DMA((2,)),
        pltpu.SemaphoreType.REGULAR((3,)),
    ]
    return pl.pallas_call(
        functools.partial(kernel, n_tm),
        out_shape=jax.ShapeDtypeStruct(args[0].shape, F32),
        in_specs=[pl.BlockSpec(memory_space=pltpu.HBM)] * 6,
        out_specs=pl.BlockSpec(memory_space=pltpu.HBM),
        scratch_shapes=scratch,
        compiler_params=pltpu.CompilerParams(
            collective_id=0, has_side_effects=True, vmem_limit_bytes=60 * 1024 * 1024
        ),
    )(*args)


def solution(mesh):
    placed = (
        P("tm", "space", None),
        P("space", None),
        P("space", None),
        P("space", None),
        P("space", None),
        P("space", None),
    )
    return jax.shard_map(
        functools.partial(body, mesh.shape["tm"]),
        mesh=mesh, in_specs=placed, out_specs=P("tm", "space", None), check_vma=False,
    )
```

```python
import functools

import jax
import jax.numpy as jnp
from jax import lax
from jax.experimental import pallas as pl
from jax.experimental.pallas import tpu as pltpu
from jax.sharding import PartitionSpec as P

M = 8
NX = 4
NZ = 8
C = 4
R = 4
T = (8, 128)
W = 128 * C
NY = 8 * R
MESH = pl.DeviceIdType.MESH
BF16 = jnp.bfloat16
F32 = jnp.float32


def tile(ref, lead, r, c):
    return ref[(*lead, pl.ds(8 * r, 8), pl.ds(128 * c, 128))]


def load_state(ref, *lead, columns=C):
    return [[tile(ref, lead, r, c) for r in range(R)] for c in range(columns)]


def store_state(ref, v, *lead):
    for c, column in enumerate(v):
        for r in range(R):
            ref[(*lead, pl.ds(8 * r, 8), pl.ds(128 * c, 128))] = column[r]


def load_win(ref, *lead):
    return load_state(ref, *lead, columns=1)[0]


def store_win(ref, v, *lead):
    store_state(ref, [v], *lead)


def add(a, b):
    if isinstance(a, list):
        return [add(x, y) for x, y in zip(a, b)]
    return a + b


def sub(a, b):
    if isinstance(a, list):
        return [sub(x, y) for x, y in zip(a, b)]
    return a - b


def iota(shape, dim):
    return lax.broadcasted_iota(jnp.int32, shape, dim)


def at_row(column, r, di):
    carry, index = divmod(r + di, R)
    x = column[index]
    return x if carry == 0 else pltpu.roll(x, (-carry) % 8, 0)


def beside(v, width):
    ext = {c: v[c] for c in range(C)}
    for j in range(1, width + 1):
        ext[-j] = [pltpu.roll(x, 1, 1) for x in v[C - j]]
        ext[C - 1 + j] = [pltpu.roll(x, 127, 1) for x in v[j - 1]]
    return ext


def advance(states, coef, first, count, source=None):
    exts = [beside(v, count) for v in states]
    for j in range(count):
        width = count - 1 - j
        news = [{} for _ in exts]
        for c in range(-width, C + width):
            for n in news:
                n[c] = []
            for r in range(R):
                k0, kl, kr, ku, kd = (tile(coef, (k,), r, c - first) for k in range(5))
                plus = None if source is None else tile(source, (), r, c)
                for n, e in zip(news, exts):
                    new = (k0 * e[c][r] + kl * e[c - 1][r]) + (kr * e[c + 1][r] + ku * at_row(e[c], r, -1))
                    new = new + kd * at_row(e[c], r, 1)
                    n[c].append(new if plus is None else new + plus)
        exts = news
    return [[e[c] for c in range(C)] for e in exts]


def two_steps(v, before, after, coef):
    def cell(e, r, c):
        k0, kl, kr, ku, kd = (tile(coef, (k,), r, c + 1) for k in range(5))
        new = (k0 * e[c][r] + kl * e[c - 1][r]) + (kr * e[c + 1][r] + ku * at_row(e[c], r, -1))
        return new + kd * at_row(e[c], r, 1)

    ext, plus = beside(v, 2), beside(before, 1)
    one = {c: [cell(ext, r, c) + plus[c][r] for r in range(R)] for c in range(-1, C + 1)}
    two = [[cell(one, r, c) + after[c][r] for r in range(R)] for c in range(C)]
    return [one[c] for c in range(C)], two


def relax(states, coef, source):
    return lax.fori_loop(0, M, lambda _, s: advance(s, coef, 0, 1, source), states)


def move(v, coef, times, count=2, unroll=1):
    def some(_, s):
        for _ in range(unroll):
            s = advance(s, coef, -1, count)
        return s

    return lax.fori_loop(0, times, some, [v])[0]


ONE = [(0, 0), (0, -1), (0, 1), (-1, 0), (1, 0)]


def sums(a, b):
    out = []
    for d in a:
        for e in b:
            f = (d[0] + e[0], d[1] + e[1])
            if f not in out:
                out.append(f)
    return out


TWO = sums(ONE, ONE)
FOUR = sums(TWO, TWO)


def along(v, dj):
    return v if dj == 0 else [pltpu.roll(x, (-dj) % 128, 1) for x in v]


def win_apply(v, coef, offsets):
    moved = {dj: along(v, dj) for dj in sorted({d[1] for d in offsets})}
    out = []
    for r in range(R):
        parts = [None] * 4
        for n, (di, dj) in enumerate(offsets):
            term = tile(coef, (n,), r, 0) * at_row(moved[dj], r, di)
            parts[n % 4] = term if parts[n % 4] is None else parts[n % 4] + term
        out.append((parts[0] + parts[1]) + (parts[2] + parts[3]))
    return out


def compose(out, a, a_offsets, b, b_offsets, out_offsets):
    seen = set()
    for dj in sorted({d[1] for d in a_offsets}):
        for n, e in enumerate(b_offsets):
            moved = along(load_win(b, n), dj)
            for m, d in enumerate(a_offsets):
                if d[1] != dj:
                    continue
                k = out_offsets.index((d[0] + e[0], d[1] + e[1]))
                for r in range(R):
                    term = tile(a, (m,), r, 0) * at_row(moved, r, d[0])
                    if k in seen:
                        term = term + tile(out, (k,), r, 0)
                    out[k, pl.ds(8 * r, 8), :] = term
                seen.add(k)


def permuted(x, matrix):
    high = x.astype(BF16)
    rest = x - high.astype(F32)
    mid = rest.astype(BF16)
    low = (rest - mid.astype(F32)).astype(BF16)
    count = x.shape[0]
    parts = jnp.concatenate([high, mid, low], axis=0)
    out = jnp.dot(parts, matrix, preferred_element_type=F32)
    return (out[:count] + out[count : 2 * count]) + out[2 * count :]


def selector(row_of_column):
    return jnp.where(iota((W, W), 0) == row_of_column, 1.0, 0.0).astype(BF16)


def inner_place(column):
    return 128 * lax.rem(column, C) + lax.div(column, C)


def merged(own, other, band):
    lane = iota(T, 1)
    low = band == 0
    out = []
    for a, b in zip(own, other):
        out.append(jnp.where(low == (lane < 64), a, b))
    return out


def kernel(
    n_tm, cpoints, initial, diffusion, velocity_x, velocity_y, source, out,
    raw, perm_in, perm_win, perm_out, c1, c8, c64, src, init, cw1, cw2, cw4, cwide, rows, cpi, rel, prl, relm, dfc,
    u_own, u_sib, u_sum, up, term, mid, lag, w1s, w1, u1, pz, t2own, t2sib, t2m, t2, rown, rsib, rm, rr, rri, t2i,
    fbuf, outi, outb, send, recv, loc, round_sem,
):
    p = lax.axis_index("tm")
    s = lax.axis_index("space")
    x = lax.rem(p, NX)
    g = lax.div(p, NX)
    z = lax.rem(g, NZ)
    y = lax.div(g, NZ)
    n_y = n_tm // (NX * NZ)
    plane = NX * NZ
    other = 1 - s
    row0 = pl.multiple_of(16 * s, 16)
    band = pl.ds(row0, 16)
    base = 4 * s
    first_slab = p == 0

    def dev(tm, space):
        return {"tm": tm, "space": space}

    def cols(c):
        return pl.ds(pl.multiple_of(128 * c, 128), 128)

    near = [dev(p, other)]
    for d in (1, NX - 1):
        near.append(dev(NX * g + lax.rem(x + d, NX), s))
    for d in (1, NZ - 1):
        near.append(dev(plane * y + NX * lax.rem(z + d, NZ) + x, s))
    for d in (1, n_y - 1):
        near.append(dev(plane * lax.rem(y + d, n_y) + NX * z + x, s))

    def tell(sem):
        for to in near:
            pl.semaphore_signal(sem, inc=1, device_id=to, device_id_type=MESH)

    def hear(sem):
        pl.semaphore_wait(sem, len(near))

    barrier = pltpu.get_barrier_semaphore()
    tell(barrier)

    fields = (diffusion, velocity_x, velocity_y, source, initial)
    for k, f in enumerate(fields):
        pltpu.make_async_copy(f, raw.at[k, band, :], loc.at[0]).start()
    pltpu.make_async_copy(cpoints.at[pl.ds(base, 4)], raw.at[pl.ds(5, 4), band, :], loc.at[0]).start()

    hear(barrier)
    tell(round_sem.at[0])

    def remote(src_ref, dst_ref, to, send_idx, recv_idx):
        return pltpu.make_async_remote_copy(
            src_ref=src_ref, dst_ref=dst_ref, send_sem=send.at[send_idx], recv_sem=recv.at[recv_idx],
            device_id=to, device_id_type=MESH,
        )

    def whole(ref, idx):
        return remote(ref, ref, dev(p, other), idx, idx)

    for k, f in enumerate(fields):
        remote(f, raw.at[k, band, :], dev(p, other), 0, 0).start()
    remote(cpoints.at[pl.ds(4 * other, 4)], raw.at[pl.ds(5, 4), band, :], dev(p, other), 0, 0).start()
    sib = whole(raw.at[pl.ds(0, 9), band, :], 0)

    line = iota((1, W), 1)
    perm_in[...] = selector(C * lax.rem(line, 128) + lax.div(line, 128))
    for ss in range(2):
        begin = 128 * lax.div(line, 128) + (64 * ss + W - 32)
        turned = lax.rem(lax.rem(line, 128) + 32 + 64 * ss, 128)
        perm_win[:, pl.ds(W * ss, W)] = selector(inner_place(lax.rem(begin + turned, W)))

    def columns_moved(first, count, at):
        moved = permuted(raw[pl.ds(first, count), pl.ds(at, 16), :].reshape(count * 16, W), perm_in[...])
        for k in range(count):
            for c in range(C):
                rows[c, pl.ds(pl.multiple_of(NY * k + at, 16), 16), :] = (
                    moved[16 * k : 16 * (k + 1), 128 * c : 128 * (c + 1)]
                )

    pltpu.make_async_copy(raw.at[pl.ds(0, 9), band, :], raw.at[pl.ds(0, 9), band, :], loc.at[0]).wait()
    columns_moved(0, 9, row0)
    sib.wait_recv()
    columns_moved(0, 9, pl.multiple_of(16 * other, 16))

    def inward(count, emit):
        for k in range(count):
            emit(k, [[rows[c, pl.ds(NY * k + r, 8, stride=R), :] for r in range(R)] for c in range(C)])

    got = {}

    def keep(k, v):
        if k < 3:
            got[k] = v
        elif k == 3:
            store_state(src, v)
        elif k == 4:
            store_state(init, v)
        else:
            store_state(cpi, v, k - 5)

    inward(9, keep)
    hear(round_sem.at[0])
    tell(round_sem.at[1])

    sub_row = iota(T, 0)
    for c in range(C):
        for r in range(R):
            d, vx, vy = (got[k][c][r] for k in range(3))
            k0 = 4.0 * d + (jnp.abs(vx) + jnp.abs(vy))
            kl = d + jnp.maximum(vx, 0.0)
            kr = d - jnp.minimum(vx, 0.0)
            ku = d + jnp.maximum(vy, 0.0)
            kd = d - jnp.minimum(vy, 0.0)
            if r == 0:
                ku = jnp.where(sub_row == 0, 0.0, ku)
            if r == R - 1:
                kd = jnp.where(sub_row == 7, 0.0, kd)
            here = (pl.ds(8 * r, 8), pl.ds(128 * c, 128))
            wide = (pl.ds(8 * r, 8), pl.ds(128 * (c + 1), 128))
            for ref, scale, at in ((c1, 1.0, here), (c8, 8.0, wide), (c64, 64.0, wide)):
                ref[(0, *at)] = 1.0 - scale * k0
                for k, val in enumerate((kl, kr, ku, kd)):
                    ref[(k + 1, *at)] = scale * val

    for ref in (c8, c64):
        for k in range(5):
            for r in range(R):
                ref[k, pl.ds(8 * r, 8), pl.ds(0, 128)] = pltpu.roll(tile(ref, (k,), r, C), 1, 1)
                ref[k, pl.ds(8 * r, 8), pl.ds(128 * (C + 1), 128)] = pltpu.roll(tile(ref, (k,), r, 1), 127, 1)

    def relax_own(extra):
        once = relax([load_state(cpi, k) for k in range(4)] + extra, c1, src)
        for k in range(4):
            store_state(rel, once[k], base + 1 + k)
        twice = relax(once, c1, src)
        for k in range(4):
            store_state(prl, twice[k], base + 1 + k)
        if extra:
            store_state(mid, twice[4])

    opens = jnp.logical_and(first_slab, s == 0)

    @pl.when(opens)
    def _():
        relax_own([load_state(init)])

    @pl.when(jnp.logical_not(opens))
    def _():
        relax_own([])
        mid[...] = jnp.zeros_like(mid)

    hear(round_sem.at[1])
    tell(round_sem.at[2])

    head = sub(load_state(mid), load_state(rel, base + 1))

    def defect(k):
        return sub(load_state(prl, base + k - 1), load_state(rel, base + k))

    head, late = advance([head, defect(4)], c8, -1, 1)
    head = add(head, defect(2))
    late = add(late, load_state(prl, base + 4))
    (head,) = advance([head], c8, -1, 1)
    store_state(fbuf, add(head, defect(3)))
    store_state(term, late)

    @pl.when(s == 0)
    def _():
        v = move(load_state(fbuf), c8, 1)
        v = move(add(v, load_state(term)), c8, 5)
        store_state(u_own, v)
        store_state(term, advance([v], c64, -1, 1)[0])

    @pl.when(s == 1)
    def _():
        a, b = lax.fori_loop(
            0, 4, lambda _, v: advance(v, c8, -1, 2), [load_state(fbuf), load_state(term)]
        )
        store_state(u_own, a)
        b = move(b, c8, 3)
        store_state(term, add(advance([a], c64, -1, 1)[0], b))

    w1s[...] = permuted(term[...], perm_win[...])
    for d in (2, 1, 3, 0):
        for flip in (0, 1):
            if d == 0 and flip == 0:
                continue
            xx, ss = lax.rem(x + d, NX), lax.rem(s + flip, 2)
            remote(w1s.at[:, cols(NX * ss + xx)], w1.at[2 * x + s], dev(NX * g + xx, ss), 2, 2).start()
    to_x = whole(w1.at[pl.ds(0, 2 * NX - 1)], 2)
    own = cols(NX * s + x)
    store_win(w1, [w1s[pl.ds(8 * r, 8), own] for r in range(R)], 2 * x + s)

    half = pl.ds(base + 1, 4)
    remote(u_own, u_sib, dev(p, other), 3, 3).start()
    remote(rel.at[half], rel.at[half], dev(p, other), 3, 3).start()
    remote(prl.at[half], prl.at[half], dev(p, other), 3, 3).start()
    shared = whole(rel, 3)

    hear(round_sem.at[2])

    @pl.when(p < n_tm - 1)
    def _():
        for ss in range(2):
            remote(cpoints.at[pl.ds(6, 2)], raw.at[pl.ds(9, 2), band, :], dev(p + 1, ss), 1, 1).start()

    ahead = whole(raw.at[pl.ds(9, 2)], 1)

    cwide[...] = permuted(
        c64[:, :, pl.ds(128, W)].reshape(5 * NY, W), perm_win[:, pl.ds(pl.multiple_of(W * s, W), W)]
    )
    for k in range(5):
        cw1[k] = cwide[pl.ds(NY * k, NY), cols(x)]
    compose(cw2, cw1, ONE, cw1, ONE, TWO)
    compose(cw4, cw2, TWO, cw2, TWO, FOUR)

    to_x.wait_recv()

    def group_term(i):
        return add(load_win(w1, 2 * i), load_win(w1, 2 * i + 1))

    a = add(win_apply(group_term(0), cw1, ONE), group_term(1))
    b = add(win_apply(group_term(2), cw1, ONE), group_term(3))
    store_win(u1, add(win_apply(a, cw2, TWO), b), z)

    for d in (4, 3, 5, 2, 6, 1, 7):
        zz = lax.rem(z + d, NZ)
        remote(u1.at[z], u1.at[z], dev(plane * y + NX * zz + x, s), 4, 16 + z).start()
    to_z = whole(u1.at[pl.ds(0, NZ - 1)], 4)

    perm_out[...] = selector(inner_place(line))
    shared.wait_recv()
    store_state(u_sum, add(load_state(u_own), load_state(u_sib)))
    to_up = remote(u_sum, up, dev(p + 1, s), 5, 5)

    @pl.when(p < n_tm - 1)
    def _():
        to_up.start()

    @pl.when(p > 0)
    def _():
        ahead.wait_recv()
        for ss in range(2):
            columns_moved(9, 2, 16 * ss)
        inward(2, lambda k, v: store_state(cpi, v, k))

    @pl.when(first_slab)
    def _():
        up[...] = jnp.zeros_like(up)
        for k in range(2):
            store_state(cpi, load_state(init), k)

    v = relax([load_state(cpi, 0), load_state(cpi, 1)], c1, src)
    store_state(relm, v[0])
    store_state(rel, v[1], 0)

    @pl.when(first_slab)
    def _():
        store_state(relm, load_state(init))

    v = relax([load_state(relm), load_state(rel, 0)], c1, src)
    store_state(dfc, sub(v[0], load_state(rel, 0)), 0)
    store_state(prl, v[1], 0)

    def climb(k, v):
        d = sub(load_state(prl, k - 1), load_state(rel, k))
        store_state(dfc, d, k)
        return add(advance([v], c8, -1, 1)[0], d)

    v = lax.fori_loop(1, M, climb, load_state(dfc, 0))

    store_state(mid, v)

    pz[...] = jnp.zeros_like(pz)

    @pl.when(z != 0)
    def _():
        remote(u1.at[0], u1.at[0], dev(p, other), 4, 16).wait_recv()

    def ascend(zz, acc):
        @pl.when(z == zz)
        def _():
            store_win(pz, acc)

        @pl.when(z != zz)
        def _():
            remote(u1.at[zz], u1.at[zz], dev(p, other), 4, 16 + zz).wait_recv()

        return add(win_apply(acc, cw4, FOUR), load_win(u1, zz))

    store_win(t2own, lax.fori_loop(1, NZ, ascend, load_win(u1, 0)))
    swap_t = remote(t2own, t2sib, dev(p, other), 7, 7)
    swap_t.start()

    acc = load_win(pz)
    store_win(rown, acc, 0)
    for i in range(NX):
        acc = add(win_apply(acc, cw1, ONE), group_term(i))
        store_win(rown, acc, i + 1)
    swap_r = remote(rown, rsib, dev(p, other), 8, 8)
    swap_r.start()

    swap_t.wait_recv()
    store_win(t2m, merged(load_win(t2own), load_win(t2sib), s))
    for yy in (2, 3, 1):
        @pl.when(yy > y)
        def _():
            for xx in range(NX):
                remote(
                    t2m, t2.at[y, :, cols(x)], dev(plane * yy + NX * z + xx, s), 8 + yy, 10 + y
                ).start()

    swap_r.wait_recv()
    for i in range(NX + 1):
        store_win(rm, merged(load_win(rown, i), load_win(rsib, i), s), i)
    to_r = []
    for i in range(NX):
        there = NX * g + 2 + i
        copy = remote(rm.at[pl.ds(i, 2)], rr.at[:, :, cols(x)], dev(there, s), 12 + i, 9)
        go = x != i + 2 if i < 2 else there < n_tm
        to_r.append((go, copy))

        @pl.when(go)
        def _():
            copy.start()

        if i < 2:
            @pl.when(x == i + 2)
            def _():
                for j in range(2):
                    rr[j, :, cols(x)] = rm[i + j]

    @pl.when(p > 0)
    def _():
        to_up.wait_recv()

    store_state(mid, add(load_state(mid), load_state(up)))
    to_lag = remote(mid, lag, dev(p + 1, s), 6, 6)

    @pl.when(p < n_tm - 1)
    def _():
        to_lag.start()

    @pl.when(p < 2)
    def _():
        rr[...] = jnp.zeros_like(rr)

    @pl.when(first_slab)
    def _():
        lag[...] = jnp.zeros_like(lag)

    q = jnp.maximum(p - 2, 0)
    n = lax.rem(q, plane)
    yq = lax.div(q, plane)
    fbuf[...] = jnp.zeros_like(fbuf)
    for yy in range(n_y - 1):
        @pl.when(yy < yq)
        def _():
            if yy > 0:
                v = move(load_state(fbuf), c64, (plane - 4) // 4, 2, 2)
            whole(t2.at[yy], 10 + yy).wait_recv()
            t2i[...] = permuted(t2[yy], perm_in[...])
            if yy > 0:
                for _ in range(2):
                    (v,) = advance([v], c64, -1, 2)
            f = load_state(t2i)
            store_state(fbuf, add(v, f) if yy > 0 else f)

    n = jnp.where(yq > 0, n, 0)
    f = move(load_state(fbuf), c64, lax.div(n, 2))
    f = move(f, c64, lax.rem(n, 2), 1)

    @pl.when(x >= 2)
    def _():
        whole(rr.at[:, :, pl.ds(0, W - 128)], 9).wait_recv()

    @pl.when(jnp.logical_and(x < 2, g > 0))
    def _():
        whole(rr, 9).wait_recv()

    @pl.when(p > 0)
    def _():
        to_lag.wait_recv()

    rri[...] = permuted(rr[...].reshape(2 * NY, W), perm_in[...]).reshape(2, NY, W)

    e = add(f, load_state(rri, 0))
    (f,) = advance([f], c64, -1, 1)
    last = add(add(f, load_state(rri, 1)), load_state(mid))

    def emit(k, value):
        for c in range(C):
            for r in range(R):
                rows[c, pl.ds(r, 8, stride=R), :] = value[c][r]
        for c in range(C):
            for t in range(2):
                outi[k, pl.ds(8 * t, 8), pl.ds(128 * c, 128)] = rows[c, pl.ds(pl.multiple_of(row0 + 8 * t, 8), 8), :]

    emit(M - 1, add(last, load_state(rel, M - 1)))

    def errors(i, v):
        k = 2 * i
        one, two = two_steps(v, load_state(dfc, k), load_state(dfc, k + 1), c8)
        emit(k, add(one, load_state(rel, k)))
        emit(k + 1, add(two, load_state(rel, k + 1)))
        return two

    v = lax.fori_loop(0, M // 2 - 1, errors, add(load_state(lag), e))
    v = add(advance([v], c8, -1, 1)[0], load_state(dfc, M - 2))
    emit(M - 2, add(v, load_state(rel, M - 2)))
    outb[...] = permuted(outi[...].reshape(M * 16, W), perm_out[...]).reshape(M, 16, W)
    done = pltpu.make_async_copy(outb, out, loc.at[1])
    done.start()

    for yy in range(n_y - 1):
        @pl.when(jnp.logical_and(yy >= yq, yy < y))
        def _():
            whole(t2.at[yy], 10 + yy).wait_recv()

    sib.wait_send()

    @pl.when(p < n_tm - 1)
    def _():
        ahead.wait_send()
        to_up.wait_send()
        to_lag.wait_send()

    for copy in (to_x, shared, to_z, swap_t, swap_r):
        copy.wait_send()
    for yy in range(1, n_y):
        @pl.when(yy > y)
        def _():
            whole(t2.at[0], 8 + yy).wait_send()

    for go, copy in to_r:
        @pl.when(go)
        def _():
            copy.wait_send()

    done.wait()


def body(n_tm, *args):
    def vmem(*shape, dtype=F32):
        return pltpu.VMEM(shape, dtype)

    def state(*lead):
        return vmem(*lead, NY, W)

    def window(*lead):
        return vmem(*lead, NY, 128)

    square = vmem(W, W, dtype=BF16)
    scratch = [
        state(11), square, vmem(W, 2 * W, dtype=BF16), square,
        state(5), vmem(5, NY, W + 256), vmem(5, NY, W + 256), state(), state(),
        window(len(ONE)), window(len(TWO)), window(len(FOUR)), vmem(5 * NY, W),
        vmem(C, 9 * NY, 128), state(4), state(9), state(9), state(), state(M),
        state(), state(), state(), state(), state(), state(), state(),
        vmem(NY, 2 * W), window(2 * NX), window(NZ), window(),
        window(), window(), window(), state(n_tm // (NX * NZ) - 1),
        window(NX + 1), window(NX + 1), window(NX + 1), state(2), state(2), state(),
        state(), vmem(M, 16, W), vmem(M, 16, W),
        pltpu.SemaphoreType.DMA((16,)), pltpu.SemaphoreType.DMA((24,)), pltpu.SemaphoreType.DMA((2,)),
        pltpu.SemaphoreType.REGULAR((3,)),
    ]
    return pl.pallas_call(
        functools.partial(kernel, n_tm),
        out_shape=jax.ShapeDtypeStruct(args[0].shape, F32),
        in_specs=[pl.BlockSpec(memory_space=pltpu.HBM)] * 6,
        out_specs=pl.BlockSpec(memory_space=pltpu.HBM),
        scratch_shapes=scratch,
        compiler_params=pltpu.CompilerParams(
            collective_id=0, has_side_effects=True, vmem_limit_bytes=60 * 1024 * 1024
        ),
    )(*args)


def solution(mesh):
    placed = (
        P("tm", "space", None),
        P("space", None),
        P("space", None),
        P("space", None),
        P("space", None),
        P("space", None),
    )
    return jax.shard_map(
        functools.partial(body, mesh.shape["tm"]),
        mesh=mesh, in_specs=placed, out_specs=P("tm", "space", None), check_vma=False,
    )
```

```python
import functools

import jax
import jax.numpy as jnp
from jax import lax
from jax.experimental import pallas as pl
from jax.experimental.pallas import tpu as pltpu
from jax.sharding import PartitionSpec as P

M = 8
NX = 4
NZ = 8
C = 4
R = 4
T = (8, 128)
W = 128 * C
NY = 8 * R
MESH = pl.DeviceIdType.MESH
BF16 = jnp.bfloat16
F32 = jnp.float32


def tile(ref, lead, r, c):
    return ref[(*lead, pl.ds(8 * r, 8), pl.ds(128 * c, 128))]


def load_state(ref, *lead, columns=C):
    return [[tile(ref, lead, r, c) for r in range(R)] for c in range(columns)]


def store_state(ref, v, *lead):
    for c, column in enumerate(v):
        for r in range(R):
            ref[(*lead, pl.ds(8 * r, 8), pl.ds(128 * c, 128))] = column[r]


def load_win(ref, *lead):
    return load_state(ref, *lead, columns=1)[0]


def store_win(ref, v, *lead):
    store_state(ref, [v], *lead)


def add(a, b):
    if isinstance(a, list):
        return [add(x, y) for x, y in zip(a, b)]
    return a + b


def sub(a, b):
    if isinstance(a, list):
        return [sub(x, y) for x, y in zip(a, b)]
    return a - b


def iota(shape, dim):
    return lax.broadcasted_iota(jnp.int32, shape, dim)


def at_row(column, r, di):
    carry, index = divmod(r + di, R)
    x = column[index]
    return x if carry == 0 else pltpu.roll(x, (-carry) % 8, 0)


def beside(v, width):
    ext = {c: v[c] for c in range(C)}
    for j in range(1, width + 1):
        ext[-j] = [pltpu.roll(x, 1, 1) for x in v[C - j]]
        ext[C - 1 + j] = [pltpu.roll(x, 127, 1) for x in v[j - 1]]
    return ext


def advance(states, coef, first, count, source=None):
    exts = [beside(v, count) for v in states]
    for j in range(count):
        width = count - 1 - j
        news = [{} for _ in exts]
        for c in range(-width, C + width):
            for n in news:
                n[c] = []
            for r in range(R):
                k0, kl, kr, ku, kd = (tile(coef, (k,), r, c - first) for k in range(5))
                plus = None if source is None else tile(source, (), r, c)
                for n, e in zip(news, exts):
                    new = (k0 * e[c][r] + kl * e[c - 1][r]) + (kr * e[c + 1][r] + ku * at_row(e[c], r, -1))
                    new = new + kd * at_row(e[c], r, 1)
                    n[c].append(new if plus is None else new + plus)
        exts = news
    return [[e[c] for c in range(C)] for e in exts]


def two_steps(v, before, after, coef):
    def cell(e, r, c):
        k0, kl, kr, ku, kd = (tile(coef, (k,), r, c + 1) for k in range(5))
        new = (k0 * e[c][r] + kl * e[c - 1][r]) + (kr * e[c + 1][r] + ku * at_row(e[c], r, -1))
        return new + kd * at_row(e[c], r, 1)

    ext, plus = beside(v, 2), beside(before, 1)
    one = {c: [cell(ext, r, c) + plus[c][r] for r in range(R)] for c in range(-1, C + 1)}
    two = [[cell(one, r, c) + after[c][r] for r in range(R)] for c in range(C)]
    return [one[c] for c in range(C)], two


def relax(states, coef, source):
    return lax.fori_loop(0, M, lambda _, s: advance(s, coef, 0, 1, source), states)


def move(v, coef, times, count=2, unroll=1):
    def some(_, s):
        for _ in range(unroll):
            s = advance(s, coef, -1, count)
        return s

    return lax.fori_loop(0, times, some, [v])[0]


ONE = [(0, 0), (0, -1), (0, 1), (-1, 0), (1, 0)]


def sums(a, b):
    out = []
    for d in a:
        for e in b:
            f = (d[0] + e[0], d[1] + e[1])
            if f not in out:
                out.append(f)
    return out


TWO = sums(ONE, ONE)
FOUR = sums(TWO, TWO)


def along(v, dj):
    return v if dj == 0 else [pltpu.roll(x, (-dj) % 128, 1) for x in v]


def win_apply(v, coef, offsets):
    moved = {dj: along(v, dj) for dj in sorted({d[1] for d in offsets})}
    out = []
    for r in range(R):
        parts = [None] * 4
        for n, (di, dj) in enumerate(offsets):
            term = tile(coef, (n,), r, 0) * at_row(moved[dj], r, di)
            parts[n % 4] = term if parts[n % 4] is None else parts[n % 4] + term
        out.append((parts[0] + parts[1]) + (parts[2] + parts[3]))
    return out


def compose(out, a, a_offsets, b, b_offsets, out_offsets):
    seen = set()
    for dj in sorted({d[1] for d in a_offsets}):
        for n, e in enumerate(b_offsets):
            moved = along(load_win(b, n), dj)
            for m, d in enumerate(a_offsets):
                if d[1] != dj:
                    continue
                k = out_offsets.index((d[0] + e[0], d[1] + e[1]))
                for r in range(R):
                    term = tile(a, (m,), r, 0) * at_row(moved, r, d[0])
                    if k in seen:
                        term = term + tile(out, (k,), r, 0)
                    out[k, pl.ds(8 * r, 8), :] = term
                seen.add(k)


def permuted(x, matrix):
    high = x.astype(BF16)
    rest = x - high.astype(F32)
    mid = rest.astype(BF16)
    low = (rest - mid.astype(F32)).astype(BF16)
    count = x.shape[0]
    parts = jnp.concatenate([high, mid, low], axis=0)
    out = jnp.dot(parts, matrix, preferred_element_type=F32)
    return (out[:count] + out[count : 2 * count]) + out[2 * count :]


def selector(row_of_column):
    return jnp.where(iota((W, W), 0) == row_of_column, 1.0, 0.0).astype(BF16)


def inner_place(column):
    return 128 * lax.rem(column, C) + lax.div(column, C)


def merged(own, other, band):
    lane = iota(T, 1)
    low = band == 0
    out = []
    for a, b in zip(own, other):
        out.append(jnp.where(low == (lane < 64), a, b))
    return out


def kernel(
    n_tm, cpoints, initial, diffusion, velocity_x, velocity_y, source, out,
    raw, perm_in, perm_win, perm_out, c1, c8, c64, src, init, cw1, cw2, cw4, cwide, rows, cpi, rel, prl, relm, dfc,
    u_own, u_sib, u_sum, up, term, mid, lag, w1s, w1, u1, pz, t2own, t2sib, t2m, t2, rown, rsib, rm, rr, rri, t2i,
    fbuf, outi, outb, send, recv, loc, round_sem,
):
    p = lax.axis_index("tm")
    s = lax.axis_index("space")
    x = lax.rem(p, NX)
    g = lax.div(p, NX)
    z = lax.rem(g, NZ)
    y = lax.div(g, NZ)
    n_y = n_tm // (NX * NZ)
    plane = NX * NZ
    other = 1 - s
    row0 = pl.multiple_of(16 * s, 16)
    band = pl.ds(row0, 16)
    base = 4 * s
    first_slab = p == 0

    def dev(tm, space):
        return {"tm": tm, "space": space}

    def cols(c):
        return pl.ds(pl.multiple_of(128 * c, 128), 128)

    near = [dev(p, other)]
    for d in (1, NX - 1):
        near.append(dev(NX * g + lax.rem(x + d, NX), s))
    for d in (1, NZ - 1):
        near.append(dev(plane * y + NX * lax.rem(z + d, NZ) + x, s))
    for d in (1, n_y - 1):
        near.append(dev(plane * lax.rem(y + d, n_y) + NX * z + x, s))

    def tell(sem):
        for to in near:
            pl.semaphore_signal(sem, inc=1, device_id=to, device_id_type=MESH)

    def hear(sem):
        pl.semaphore_wait(sem, len(near))

    barrier = pltpu.get_barrier_semaphore()
    tell(barrier)

    fields = (diffusion, velocity_x, velocity_y, source, initial)
    for k, f in enumerate(fields):
        pltpu.make_async_copy(f, raw.at[k, band, :], loc.at[0]).start()
    pltpu.make_async_copy(cpoints.at[pl.ds(base, 4)], raw.at[pl.ds(5, 4), band, :], loc.at[0]).start()

    hear(barrier)
    tell(round_sem.at[0])

    def remote(src_ref, dst_ref, to, send_idx, recv_idx):
        return pltpu.make_async_remote_copy(
            src_ref=src_ref, dst_ref=dst_ref, send_sem=send.at[send_idx], recv_sem=recv.at[recv_idx],
            device_id=to, device_id_type=MESH,
        )

    def whole(ref, idx):
        return remote(ref, ref, dev(p, other), idx, idx)

    for k, f in enumerate(fields):
        remote(f, raw.at[k, band, :], dev(p, other), 0, 0).start()
    remote(cpoints.at[pl.ds(4 * other, 4)], raw.at[pl.ds(5, 4), band, :], dev(p, other), 0, 0).start()
    sib = whole(raw.at[pl.ds(0, 9), band, :], 0)

    line = iota((1, W), 1)
    perm_in[...] = selector(C * lax.rem(line, 128) + lax.div(line, 128))
    for ss in range(2):
        begin = 128 * lax.div(line, 128) + (64 * ss + W - 32)
        turned = lax.rem(lax.rem(line, 128) + 32 + 64 * ss, 128)
        perm_win[:, pl.ds(W * ss, W)] = selector(inner_place(lax.rem(begin + turned, W)))

    def columns_moved(first, count, at):
        moved = permuted(raw[pl.ds(first, count), pl.ds(at, 16), :].reshape(count * 16, W), perm_in[...])
        for k in range(count):
            for c in range(C):
                rows[c, pl.ds(pl.multiple_of(NY * k + at, 16), 16), :] = (
                    moved[16 * k : 16 * (k + 1), 128 * c : 128 * (c + 1)]
                )

    pltpu.make_async_copy(raw.at[pl.ds(0, 9), band, :], raw.at[pl.ds(0, 9), band, :], loc.at[0]).wait()
    columns_moved(0, 9, row0)
    sib.wait_recv()
    columns_moved(0, 9, pl.multiple_of(16 * other, 16))

    def inward(count, emit):
        for k in range(count):
            emit(k, [[rows[c, pl.ds(NY * k + r, 8, stride=R), :] for r in range(R)] for c in range(C)])

    got = {}

    def keep(k, v):
        if k < 3:
            got[k] = v
        elif k == 3:
            store_state(src, v)
        elif k == 4:
            store_state(init, v)
        else:
            store_state(cpi, v, k - 5)

    inward(9, keep)
    hear(round_sem.at[0])
    tell(round_sem.at[1])

    sub_row = iota(T, 0)
    for c in range(C):
        for r in range(R):
            d, vx, vy = (got[k][c][r] for k in range(3))
            k0 = 4.0 * d + (jnp.abs(vx) + jnp.abs(vy))
            kl = d + jnp.maximum(vx, 0.0)
            kr = d - jnp.minimum(vx, 0.0)
            ku = d + jnp.maximum(vy, 0.0)
            kd = d - jnp.minimum(vy, 0.0)
            if r == 0:
                ku = jnp.where(sub_row == 0, 0.0, ku)
            if r == R - 1:
                kd = jnp.where(sub_row == 7, 0.0, kd)
            here = (pl.ds(8 * r, 8), pl.ds(128 * c, 128))
            wide = (pl.ds(8 * r, 8), pl.ds(128 * (c + 1), 128))
            for ref, scale, at in ((c1, 1.0, here), (c8, 8.0, wide), (c64, 64.0, wide)):
                ref[(0, *at)] = 1.0 - scale * k0
                for k, val in enumerate((kl, kr, ku, kd)):
                    ref[(k + 1, *at)] = scale * val

    for ref in (c8, c64):
        for k in range(5):
            for r in range(R):
                ref[k, pl.ds(8 * r, 8), pl.ds(0, 128)] = pltpu.roll(tile(ref, (k,), r, C), 1, 1)
                ref[k, pl.ds(8 * r, 8), pl.ds(128 * (C + 1), 128)] = pltpu.roll(tile(ref, (k,), r, 1), 127, 1)

    def relax_own(extra):
        once = relax([load_state(cpi, k) for k in range(4)] + extra, c1, src)
        for k in range(4):
            store_state(rel, once[k], base + 1 + k)
        twice = relax(once, c1, src)
        for k in range(4):
            store_state(prl, twice[k], base + 1 + k)
        if extra:
            store_state(mid, twice[4])

    opens = jnp.logical_and(first_slab, s == 0)

    @pl.when(opens)
    def _():
        relax_own([load_state(init)])

    @pl.when(jnp.logical_not(opens))
    def _():
        relax_own([])
        mid[...] = jnp.zeros_like(mid)

    hear(round_sem.at[1])
    tell(round_sem.at[2])

    head = sub(load_state(mid), load_state(rel, base + 1))

    def defect(k):
        return sub(load_state(prl, base + k - 1), load_state(rel, base + k))

    head, late = advance([head, defect(4)], c8, -1, 1)
    head = add(head, defect(2))
    late = add(late, load_state(prl, base + 4))
    (head,) = advance([head], c8, -1, 1)
    store_state(fbuf, add(head, defect(3)))
    store_state(term, late)

    @pl.when(s == 0)
    def _():
        v = move(load_state(fbuf), c8, 1)
        v = move(add(v, load_state(term)), c8, 5)
        store_state(u_own, v)
        store_state(term, advance([v], c64, -1, 1)[0])

    @pl.when(s == 1)
    def _():
        a, b = lax.fori_loop(
            0, 4, lambda _, v: advance(v, c8, -1, 2), [load_state(fbuf), load_state(term)]
        )
        store_state(u_own, a)
        b = move(b, c8, 3)
        store_state(term, add(advance([a], c64, -1, 1)[0], b))

    w1s[...] = permuted(term[...], perm_win[...])
    for d in (2, 1, 3, 0):
        for flip in (0, 1):
            if d == 0 and flip == 0:
                continue
            xx, ss = lax.rem(x + d, NX), lax.rem(s + flip, 2)
            remote(w1s.at[:, cols(NX * ss + xx)], w1.at[2 * x + s], dev(NX * g + xx, ss), 2, 2).start()
    to_x = whole(w1.at[pl.ds(0, 2 * NX - 1)], 2)
    own = cols(NX * s + x)
    store_win(w1, [w1s[pl.ds(8 * r, 8), own] for r in range(R)], 2 * x + s)

    half = pl.ds(base + 1, 4)
    remote(u_own, u_sib, dev(p, other), 3, 3).start()
    remote(rel.at[half], rel.at[half], dev(p, other), 3, 3).start()
    remote(prl.at[half], prl.at[half], dev(p, other), 3, 3).start()
    shared = whole(rel, 3)

    hear(round_sem.at[2])

    @pl.when(p < n_tm - 1)
    def _():
        for ss in range(2):
            remote(cpoints.at[pl.ds(6, 2)], raw.at[pl.ds(9, 2), band, :], dev(p + 1, ss), 1, 1).start()

    ahead = whole(raw.at[pl.ds(9, 2)], 1)

    cwide[...] = permuted(
        c64[:, :, pl.ds(128, W)].reshape(5 * NY, W), perm_win[:, pl.ds(pl.multiple_of(W * s, W), W)]
    )
    for k in range(5):
        cw1[k] = cwide[pl.ds(NY * k, NY), cols(x)]
    compose(cw2, cw1, ONE, cw1, ONE, TWO)
    compose(cw4, cw2, TWO, cw2, TWO, FOUR)

    to_x.wait_recv()

    def group_term(i):
        return add(load_win(w1, 2 * i), load_win(w1, 2 * i + 1))

    a = add(win_apply(group_term(0), cw1, ONE), group_term(1))
    b = add(win_apply(group_term(2), cw1, ONE), group_term(3))
    store_win(u1, add(win_apply(a, cw2, TWO), b), z)

    for d in (4, 3, 5, 2, 6, 1, 7):
        zz = lax.rem(z + d, NZ)
        remote(u1.at[z], u1.at[z], dev(plane * y + NX * zz + x, s), 4, 16 + z).start()
    to_z = whole(u1.at[pl.ds(0, NZ - 1)], 4)

    perm_out[...] = selector(inner_place(line))
    shared.wait_recv()
    store_state(u_sum, add(load_state(u_own), load_state(u_sib)))
    to_up = remote(u_sum, up, dev(p + 1, s), 5, 5)

    @pl.when(p < n_tm - 1)
    def _():
        to_up.start()

    pz[...] = jnp.zeros_like(pz)

    @pl.when(z != 0)
    def _():
        remote(u1.at[0], u1.at[0], dev(p, other), 4, 16).wait_recv()

    def ascend(zz, acc):
        @pl.when(z == zz)
        def _():
            store_win(pz, acc)

        @pl.when(z != zz)
        def _():
            remote(u1.at[zz], u1.at[zz], dev(p, other), 4, 16 + zz).wait_recv()

        return add(win_apply(acc, cw4, FOUR), load_win(u1, zz))

    store_win(t2own, lax.fori_loop(1, NZ, ascend, load_win(u1, 0)))
    swap_t = remote(t2own, t2sib, dev(p, other), 7, 7)
    swap_t.start()

    acc = load_win(pz)
    store_win(rown, acc, 0)
    for i in range(NX):
        acc = add(win_apply(acc, cw1, ONE), group_term(i))
        store_win(rown, acc, i + 1)
    swap_r = remote(rown, rsib, dev(p, other), 8, 8)
    swap_r.start()

    swap_t.wait_recv()
    store_win(t2m, merged(load_win(t2own), load_win(t2sib), s))
    for yy in (2, 3, 1):
        @pl.when(yy > y)
        def _():
            for xx in range(NX):
                remote(
                    t2m, t2.at[y, :, cols(x)], dev(plane * yy + NX * z + xx, s), 8 + yy, 10 + y
                ).start()

    swap_r.wait_recv()
    for i in range(NX + 1):
        store_win(rm, merged(load_win(rown, i), load_win(rsib, i), s), i)
    to_r = []
    for i in range(NX):
        there = NX * g + 2 + i
        copy = remote(rm.at[pl.ds(i, 2)], rr.at[:, :, cols(x)], dev(there, s), 12 + i, 9)
        go = x != i + 2 if i < 2 else there < n_tm
        to_r.append((go, copy))

        @pl.when(go)
        def _():
            copy.start()

        if i < 2:
            @pl.when(x == i + 2)
            def _():
                for j in range(2):
                    rr[j, :, cols(x)] = rm[i + j]

    @pl.when(p > 0)
    def _():
        ahead.wait_recv()
        for ss in range(2):
            columns_moved(9, 2, 16 * ss)
        inward(2, lambda k, v: store_state(cpi, v, k))

    @pl.when(first_slab)
    def _():
        up[...] = jnp.zeros_like(up)
        for k in range(2):
            store_state(cpi, load_state(init), k)

    v = relax([load_state(cpi, 0), load_state(cpi, 1)], c1, src)
    store_state(relm, v[0])
    store_state(rel, v[1], 0)

    @pl.when(first_slab)
    def _():
        store_state(relm, load_state(init))

    v = relax([load_state(relm), load_state(rel, 0)], c1, src)
    store_state(dfc, sub(v[0], load_state(rel, 0)), 0)
    store_state(prl, v[1], 0)

    def climb(k, v):
        d = sub(load_state(prl, k - 1), load_state(rel, k))
        store_state(dfc, d, k)
        return add(advance([v], c8, -1, 1)[0], d)

    v = lax.fori_loop(1, M, climb, load_state(dfc, 0))

    store_state(mid, v)

    @pl.when(p > 0)
    def _():
        to_up.wait_recv()

    store_state(mid, add(load_state(mid), load_state(up)))
    to_lag = remote(mid, lag, dev(p + 1, s), 6, 6)

    @pl.when(p < n_tm - 1)
    def _():
        to_lag.start()

    @pl.when(p < 2)
    def _():
        rr[...] = jnp.zeros_like(rr)

    @pl.when(first_slab)
    def _():
        lag[...] = jnp.zeros_like(lag)

    q = jnp.maximum(p - 2, 0)
    n = lax.rem(q, plane)
    yq = lax.div(q, plane)
    fbuf[...] = jnp.zeros_like(fbuf)
    for yy in range(n_y - 1):
        @pl.when(yy < yq)
        def _():
            if yy > 0:
                v = move(load_state(fbuf), c64, (plane - 4) // 4, 2, 2)
            whole(t2.at[yy], 10 + yy).wait_recv()
            t2i[...] = permuted(t2[yy], perm_in[...])
            if yy > 0:
                for _ in range(2):
                    (v,) = advance([v], c64, -1, 2)
            f = load_state(t2i)
            store_state(fbuf, add(v, f) if yy > 0 else f)

    n = jnp.where(yq > 0, n, 0)
    f = move(load_state(fbuf), c64, lax.div(n, 2))
    f = move(f, c64, lax.rem(n, 2), 1)

    @pl.when(x >= 2)
    def _():
        whole(rr.at[:, :, pl.ds(0, W - 128)], 9).wait_recv()

    @pl.when(jnp.logical_and(x < 2, g > 0))
    def _():
        whole(rr, 9).wait_recv()

    @pl.when(p > 0)
    def _():
        to_lag.wait_recv()

    rri[...] = permuted(rr[...].reshape(2 * NY, W), perm_in[...]).reshape(2, NY, W)

    e = add(f, load_state(rri, 0))
    (f,) = advance([f], c64, -1, 1)
    last = add(add(f, load_state(rri, 1)), load_state(mid))

    def emit(k, value):
        for c in range(C):
            for r in range(R):
                rows[c, pl.ds(r, 8, stride=R), :] = value[c][r]
        for c in range(C):
            for t in range(2):
                outi[k, pl.ds(8 * t, 8), pl.ds(128 * c, 128)] = rows[c, pl.ds(pl.multiple_of(row0 + 8 * t, 8), 8), :]

    emit(M - 1, add(last, load_state(rel, M - 1)))

    def errors(i, v):
        k = 2 * i
        one, two = two_steps(v, load_state(dfc, k), load_state(dfc, k + 1), c8)
        emit(k, add(one, load_state(rel, k)))
        emit(k + 1, add(two, load_state(rel, k + 1)))
        return two

    v = lax.fori_loop(0, M // 2 - 1, errors, add(load_state(lag), e))
    v = add(advance([v], c8, -1, 1)[0], load_state(dfc, M - 2))
    emit(M - 2, add(v, load_state(rel, M - 2)))
    outb[...] = permuted(outi[...].reshape(M * 16, W), perm_out[...]).reshape(M, 16, W)
    done = pltpu.make_async_copy(outb, out, loc.at[1])
    done.start()

    for yy in range(n_y - 1):
        @pl.when(jnp.logical_and(yy >= yq, yy < y))
        def _():
            whole(t2.at[yy], 10 + yy).wait_recv()

    sib.wait_send()

    @pl.when(p < n_tm - 1)
    def _():
        ahead.wait_send()
        to_up.wait_send()
        to_lag.wait_send()

    for copy in (to_x, shared, to_z, swap_t, swap_r):
        copy.wait_send()
    for yy in range(1, n_y):
        @pl.when(yy > y)
        def _():
            whole(t2.at[0], 8 + yy).wait_send()

    for go, copy in to_r:
        @pl.when(go)
        def _():
            copy.wait_send()

    done.wait()


def body(n_tm, *args):
    def vmem(*shape, dtype=F32):
        return pltpu.VMEM(shape, dtype)

    def state(*lead):
        return vmem(*lead, NY, W)

    def window(*lead):
        return vmem(*lead, NY, 128)

    square = vmem(W, W, dtype=BF16)
    scratch = [
        state(11), square, vmem(W, 2 * W, dtype=BF16), square,
        state(5), vmem(5, NY, W + 256), vmem(5, NY, W + 256), state(), state(),
        window(len(ONE)), window(len(TWO)), window(len(FOUR)), vmem(5 * NY, W),
        vmem(C, 9 * NY, 128), state(4), state(9), state(9), state(), state(M),
        state(), state(), state(), state(), state(), state(), state(),
        vmem(NY, 2 * W), window(2 * NX), window(NZ), window(),
        window(), window(), window(), state(n_tm // (NX * NZ) - 1),
        window(NX + 1), window(NX + 1), window(NX + 1), state(2), state(2), state(),
        state(), vmem(M, 16, W), vmem(M, 16, W),
        pltpu.SemaphoreType.DMA((16,)), pltpu.SemaphoreType.DMA((24,)), pltpu.SemaphoreType.DMA((2,)),
        pltpu.SemaphoreType.REGULAR((3,)),
    ]
    return pl.pallas_call(
        functools.partial(kernel, n_tm),
        out_shape=jax.ShapeDtypeStruct(args[0].shape, F32),
        in_specs=[pl.BlockSpec(memory_space=pltpu.HBM)] * 6,
        out_specs=pl.BlockSpec(memory_space=pltpu.HBM),
        scratch_shapes=scratch,
        compiler_params=pltpu.CompilerParams(
            collective_id=0, has_side_effects=True, vmem_limit_bytes=60 * 1024 * 1024
        ),
    )(*args)


def solution(mesh):
    placed = (
        P("tm", "space", None),
        P("space", None),
        P("space", None),
        P("space", None),
        P("space", None),
        P("space", None),
    )
    return jax.shard_map(
        functools.partial(body, mesh.shape["tm"]),
        mesh=mesh, in_specs=placed, out_specs=P("tm", "space", None), check_vma=False,
    )
```

```python
import functools

import jax
import jax.numpy as jnp
from jax import lax
from jax.experimental import pallas as pl
from jax.experimental.pallas import tpu as pltpu
from jax.sharding import PartitionSpec as P

M = 8
NX = 4
NZ = 8
C = 4
R = 4
T = (8, 128)
W = 128 * C
NY = 8 * R
MESH = pl.DeviceIdType.MESH
BF16 = jnp.bfloat16
F32 = jnp.float32


def tile(ref, lead, r, c):
    return ref[(*lead, pl.ds(8 * r, 8), pl.ds(128 * c, 128))]


def load_state(ref, *lead, columns=C):
    return [[tile(ref, lead, r, c) for r in range(R)] for c in range(columns)]


def store_state(ref, v, *lead):
    for c, column in enumerate(v):
        for r in range(R):
            ref[(*lead, pl.ds(8 * r, 8), pl.ds(128 * c, 128))] = column[r]


def load_win(ref, *lead):
    return load_state(ref, *lead, columns=1)[0]


def store_win(ref, v, *lead):
    store_state(ref, [v], *lead)


def add(a, b):
    if isinstance(a, list):
        return [add(x, y) for x, y in zip(a, b)]
    return a + b


def sub(a, b):
    if isinstance(a, list):
        return [sub(x, y) for x, y in zip(a, b)]
    return a - b


def iota(shape, dim):
    return lax.broadcasted_iota(jnp.int32, shape, dim)


def at_row(column, r, di):
    carry, index = divmod(r + di, R)
    x = column[index]
    return x if carry == 0 else pltpu.roll(x, (-carry) % 8, 0)


def beside(v, width):
    ext = {c: v[c] for c in range(C)}
    for j in range(1, width + 1):
        ext[-j] = [pltpu.roll(x, 1, 1) for x in v[C - j]]
        ext[C - 1 + j] = [pltpu.roll(x, 127, 1) for x in v[j - 1]]
    return ext


def advance(states, coef, first, count, source=None):
    exts = [beside(v, count) for v in states]
    for j in range(count):
        width = count - 1 - j
        news = [{} for _ in exts]
        for c in range(-width, C + width):
            for n in news:
                n[c] = []
            for r in range(R):
                k0, kl, kr, ku, kd = (tile(coef, (k,), r, c - first) for k in range(5))
                plus = None if source is None else tile(source, (), r, c)
                for n, e in zip(news, exts):
                    new = (k0 * e[c][r] + kl * e[c - 1][r]) + (kr * e[c + 1][r] + ku * at_row(e[c], r, -1))
                    new = new + kd * at_row(e[c], r, 1)
                    n[c].append(new if plus is None else new + plus)
        exts = news
    return [[e[c] for c in range(C)] for e in exts]


def two_steps(v, before, after, coef):
    def cell(e, r, c):
        k0, kl, kr, ku, kd = (tile(coef, (k,), r, c + 1) for k in range(5))
        new = (k0 * e[c][r] + kl * e[c - 1][r]) + (kr * e[c + 1][r] + ku * at_row(e[c], r, -1))
        return new + kd * at_row(e[c], r, 1)

    ext, plus = beside(v, 2), beside(before, 1)
    one = {c: [cell(ext, r, c) + plus[c][r] for r in range(R)] for c in range(-1, C + 1)}
    two = [[cell(one, r, c) + after[c][r] for r in range(R)] for c in range(C)]
    return [one[c] for c in range(C)], two


def relax(states, coef, source):
    return lax.fori_loop(0, M, lambda _, s: advance(s, coef, 0, 1, source), states)


def move(v, coef, times, count=2, unroll=1):
    def some(_, s):
        for _ in range(unroll):
            s = advance(s, coef, -1, count)
        return s

    return lax.fori_loop(0, times, some, [v])[0]


ONE = [(0, 0), (0, -1), (0, 1), (-1, 0), (1, 0)]


def sums(a, b):
    out = []
    for d in a:
        for e in b:
            f = (d[0] + e[0], d[1] + e[1])
            if f not in out:
                out.append(f)
    return out


TWO = sums(ONE, ONE)
FOUR = sums(TWO, TWO)


def along(v, dj):
    return v if dj == 0 else [pltpu.roll(x, (-dj) % 128, 1) for x in v]


def win_apply(v, coef, offsets):
    moved = {dj: along(v, dj) for dj in sorted({d[1] for d in offsets})}
    out = []
    for r in range(R):
        parts = [None] * 4
        for n, (di, dj) in enumerate(offsets):
            term = tile(coef, (n,), r, 0) * at_row(moved[dj], r, di)
            parts[n % 4] = term if parts[n % 4] is None else parts[n % 4] + term
        out.append((parts[0] + parts[1]) + (parts[2] + parts[3]))
    return out


def compose(out, a, a_offsets, b, b_offsets, out_offsets):
    seen = set()
    for dj in sorted({d[1] for d in a_offsets}):
        for n, e in enumerate(b_offsets):
            moved = along(load_win(b, n), dj)
            for m, d in enumerate(a_offsets):
                if d[1] != dj:
                    continue
                k = out_offsets.index((d[0] + e[0], d[1] + e[1]))
                for r in range(R):
                    term = tile(a, (m,), r, 0) * at_row(moved, r, d[0])
                    if k in seen:
                        term = term + tile(out, (k,), r, 0)
                    out[k, pl.ds(8 * r, 8), :] = term
                seen.add(k)


def permuted(x, matrix):
    high = x.astype(BF16)
    rest = x - high.astype(F32)
    mid = rest.astype(BF16)
    low = (rest - mid.astype(F32)).astype(BF16)
    count = x.shape[0]
    parts = jnp.concatenate([high, mid, low], axis=0)
    out = jnp.dot(parts, matrix, preferred_element_type=F32)
    return (out[:count] + out[count : 2 * count]) + out[2 * count :]


def selector(row_of_column):
    return jnp.where(iota((W, W), 0) == row_of_column, 1.0, 0.0).astype(BF16)


def inner_place(column):
    return 128 * lax.rem(column, C) + lax.div(column, C)


def merged(own, other, band):
    lane = iota(T, 1)
    low = band == 0
    out = []
    for a, b in zip(own, other):
        out.append(jnp.where(low == (lane < 64), a, b))
    return out


def kernel(
    n_tm, cpoints, initial, diffusion, velocity_x, velocity_y, source, out,
    raw, perm_in, perm_win, perm_out, c1, c8, c64, src, init, cw1, cw2, cw4, cwide, rows, cpi, rel, prl, relm, dfc,
    u_own, u_sib, u_sum, up, term, mid, lag, w1s, w1, u1, pz, t2own, t2sib, t2m, t2, rown, rsib, rm, rr, rri, t2i,
    fbuf, outi, outb, send, recv, loc, round_sem,
):
    p = lax.axis_index("tm")
    s = lax.axis_index("space")
    x = lax.rem(p, NX)
    g = lax.div(p, NX)
    z = lax.rem(g, NZ)
    y = lax.div(g, NZ)
    n_y = n_tm // (NX * NZ)
    plane = NX * NZ
    other = 1 - s
    row0 = pl.multiple_of(16 * s, 16)
    band = pl.ds(row0, 16)
    base = 4 * s
    first_slab = p == 0

    def dev(tm, space):
        return {"tm": tm, "space": space}

    def cols(c):
        return pl.ds(pl.multiple_of(128 * c, 128), 128)

    near = [dev(p, other)]
    for d in (1, NX - 1):
        near.append(dev(NX * g + lax.rem(x + d, NX), s))
    for d in (1, NZ - 1):
        near.append(dev(plane * y + NX * lax.rem(z + d, NZ) + x, s))
    for d in (1, n_y - 1):
        near.append(dev(plane * lax.rem(y + d, n_y) + NX * z + x, s))

    def tell(sem):
        for to in near:
            pl.semaphore_signal(sem, inc=1, device_id=to, device_id_type=MESH)

    def hear(sem):
        pl.semaphore_wait(sem, len(near))

    barrier = pltpu.get_barrier_semaphore()
    tell(barrier)

    fields = (diffusion, velocity_x, velocity_y, source, initial)
    for k, f in enumerate(fields):
        pltpu.make_async_copy(f, raw.at[k, band, :], loc.at[0]).start()
    pltpu.make_async_copy(cpoints.at[pl.ds(base, 4)], raw.at[pl.ds(5, 4), band, :], loc.at[0]).start()

    hear(barrier)
    tell(round_sem.at[0])

    def remote(src_ref, dst_ref, to, send_idx, recv_idx):
        return pltpu.make_async_remote_copy(
            src_ref=src_ref, dst_ref=dst_ref, send_sem=send.at[send_idx], recv_sem=recv.at[recv_idx],
            device_id=to, device_id_type=MESH,
        )

    def whole(ref, idx):
        return remote(ref, ref, dev(p, other), idx, idx)

    for k, f in enumerate(fields):
        remote(f, raw.at[k, band, :], dev(p, other), 0, 0).start()
    remote(cpoints.at[pl.ds(4 * other, 4)], raw.at[pl.ds(5, 4), band, :], dev(p, other), 0, 0).start()
    sib = whole(raw.at[pl.ds(0, 9), band, :], 0)

    line = iota((1, W), 1)
    perm_in[...] = selector(C * lax.rem(line, 128) + lax.div(line, 128))
    for ss in range(2):
        begin = 128 * lax.div(line, 128) + (64 * ss + W - 32)
        turned = lax.rem(lax.rem(line, 128) + 32 + 64 * ss, 128)
        perm_win[:, pl.ds(W * ss, W)] = selector(inner_place(lax.rem(begin + turned, W)))

    def columns_moved(first, count, at):
        moved = permuted(raw[pl.ds(first, count), pl.ds(at, 16), :].reshape(count * 16, W), perm_in[...])
        for k in range(count):
            for c in range(C):
                rows[c, pl.ds(pl.multiple_of(NY * k + at, 16), 16), :] = (
                    moved[16 * k : 16 * (k + 1), 128 * c : 128 * (c + 1)]
                )

    pltpu.make_async_copy(raw.at[pl.ds(0, 9), band, :], raw.at[pl.ds(0, 9), band, :], loc.at[0]).wait()
    columns_moved(0, 9, row0)
    sib.wait_recv()
    columns_moved(0, 9, pl.multiple_of(16 * other, 16))

    def inward(count, emit):
        for k in range(count):
            emit(k, [[rows[c, pl.ds(NY * k + r, 8, stride=R), :] for r in range(R)] for c in range(C)])

    got = {}

    def keep(k, v):
        if k < 3:
            got[k] = v
        elif k == 3:
            store_state(src, v)
        elif k == 4:
            store_state(init, v)
        else:
            store_state(cpi, v, k - 5)

    inward(9, keep)
    hear(round_sem.at[0])
    tell(round_sem.at[1])

    sub_row = iota(T, 0)
    for c in range(C):
        for r in range(R):
            d, vx, vy = (got[k][c][r] for k in range(3))
            k0 = 4.0 * d + (jnp.abs(vx) + jnp.abs(vy))
            kl = d + jnp.maximum(vx, 0.0)
            kr = d - jnp.minimum(vx, 0.0)
            ku = d + jnp.maximum(vy, 0.0)
            kd = d - jnp.minimum(vy, 0.0)
            if r == 0:
                ku = jnp.where(sub_row == 0, 0.0, ku)
            if r == R - 1:
                kd = jnp.where(sub_row == 7, 0.0, kd)
            here = (pl.ds(8 * r, 8), pl.ds(128 * c, 128))
            wide = (pl.ds(8 * r, 8), pl.ds(128 * (c + 1), 128))
            for ref, scale, at in ((c1, 1.0, here), (c8, 8.0, wide), (c64, 64.0, wide)):
                ref[(0, *at)] = 1.0 - scale * k0
                for k, val in enumerate((kl, kr, ku, kd)):
                    ref[(k + 1, *at)] = scale * val

    for ref in (c8, c64):
        for k in range(5):
            for r in range(R):
                ref[k, pl.ds(8 * r, 8), pl.ds(0, 128)] = pltpu.roll(tile(ref, (k,), r, C), 1, 1)
                ref[k, pl.ds(8 * r, 8), pl.ds(128 * (C + 1), 128)] = pltpu.roll(tile(ref, (k,), r, 1), 127, 1)

    def relax_own(extra):
        once = relax([load_state(cpi, k) for k in range(4)] + extra, c1, src)
        for k in range(4):
            store_state(rel, once[k], base + 1 + k)
        twice = relax(once, c1, src)
        for k in range(4):
            store_state(prl, twice[k], base + 1 + k)
        if extra:
            store_state(mid, twice[4])

    opens = jnp.logical_and(first_slab, s == 0)

    @pl.when(opens)
    def _():
        relax_own([load_state(init)])

    @pl.when(jnp.logical_not(opens))
    def _():
        relax_own([])
        mid[...] = jnp.zeros_like(mid)

    hear(round_sem.at[1])
    tell(round_sem.at[2])

    head = sub(load_state(mid), load_state(rel, base + 1))

    def defect(k):
        return sub(load_state(prl, base + k - 1), load_state(rel, base + k))

    head, late = advance([head, defect(4)], c8, -1, 1)
    head = add(head, defect(2))
    late = add(late, load_state(prl, base + 4))
    (head,) = advance([head], c8, -1, 1)
    store_state(fbuf, add(head, defect(3)))
    store_state(term, late)

    @pl.when(s == 0)
    def _():
        v = move(load_state(fbuf), c8, 1)
        v = move(add(v, load_state(term)), c8, 5)
        store_state(u_own, v)
        store_state(term, advance([v], c64, -1, 1)[0])

    @pl.when(s == 1)
    def _():
        a, b = lax.fori_loop(
            0, 4, lambda _, v: advance(v, c8, -1, 2), [load_state(fbuf), load_state(term)]
        )
        store_state(u_own, a)
        b = move(b, c8, 3)
        store_state(term, add(advance([a], c64, -1, 1)[0], b))

    w1s[...] = permuted(term[...], perm_win[...])
    for d in (2, 1, 3, 0):
        for flip in (0, 1):
            if d == 0 and flip == 0:
                continue
            xx, ss = lax.rem(x + d, NX), lax.rem(s + flip, 2)
            remote(w1s.at[:, cols(NX * ss + xx)], w1.at[2 * x + s], dev(NX * g + xx, ss), 2, 2).start()
    to_x = whole(w1.at[pl.ds(0, 2 * NX - 1)], 2)
    own = cols(NX * s + x)
    store_win(w1, [w1s[pl.ds(8 * r, 8), own] for r in range(R)], 2 * x + s)

    half = pl.ds(base + 1, 4)
    remote(u_own, u_sib, dev(p, other), 3, 3).start()
    remote(rel.at[half], rel.at[half], dev(p, other), 3, 3).start()
    remote(prl.at[half], prl.at[half], dev(p, other), 3, 3).start()
    shared = whole(rel, 3)

    hear(round_sem.at[2])

    @pl.when(p < n_tm - 1)
    def _():
        for ss in range(2):
            remote(cpoints.at[pl.ds(6, 2)], raw.at[pl.ds(9, 2), band, :], dev(p + 1, ss), 1, 1).start()

    ahead = whole(raw.at[pl.ds(9, 2)], 1)

    cwide[...] = permuted(
        c64[:, :, pl.ds(128, W)].reshape(5 * NY, W), perm_win[:, pl.ds(pl.multiple_of(W * s, W), W)]
    )
    for k in range(5):
        cw1[k] = cwide[pl.ds(NY * k, NY), cols(x)]
    compose(cw2, cw1, ONE, cw1, ONE, TWO)
    compose(cw4, cw2, TWO, cw2, TWO, FOUR)

    to_x.wait_recv()

    def group_term(i):
        return add(load_win(w1, 2 * i), load_win(w1, 2 * i + 1))

    a = add(win_apply(group_term(0), cw1, ONE), group_term(1))
    b = add(win_apply(group_term(2), cw1, ONE), group_term(3))
    store_win(u1, add(win_apply(a, cw2, TWO), b), z)

    for d in (4, 3, 5, 2, 6, 1, 7):
        zz = lax.rem(z + d, NZ)
        remote(u1.at[z], u1.at[z], dev(plane * y + NX * zz + x, s), 4, 16 + z).start()
    to_z = whole(u1.at[pl.ds(0, NZ - 1)], 4)

    perm_out[...] = selector(inner_place(line))
    shared.wait_recv()
    store_state(u_sum, add(load_state(u_own), load_state(u_sib)))
    to_up = remote(u_sum, up, dev(p + 1, s), 5, 5)

    @pl.when(p < n_tm - 1)
    def _():
        to_up.start()

    pz[...] = jnp.zeros_like(pz)

    @pl.when(z != 0)
    def _():
        remote(u1.at[0], u1.at[0], dev(p, other), 4, 16).wait_recv()

    def ascend(zz, acc):
        @pl.when(z == zz)
        def _():
            store_win(pz, acc)

        @pl.when(z != zz)
        def _():
            remote(u1.at[zz], u1.at[zz], dev(p, other), 4, 16 + zz).wait_recv()

        return add(win_apply(acc, cw4, FOUR), load_win(u1, zz))

    store_win(t2own, lax.fori_loop(1, NZ, ascend, load_win(u1, 0)))
    swap_t = remote(t2own, t2sib, dev(p, other), 7, 7)
    swap_t.start()

    acc = load_win(pz)
    store_win(rown, acc, 0)
    for i in range(NX):
        acc = add(win_apply(acc, cw1, ONE), group_term(i))
        store_win(rown, acc, i + 1)
    swap_r = remote(rown, rsib, dev(p, other), 8, 8)
    swap_r.start()

    swap_t.wait_recv()
    store_win(t2m, merged(load_win(t2own), load_win(t2sib), s))
    for yy in (2, 3, 1):
        @pl.when(yy > y)
        def _():
            for xx in range(NX):
                remote(
                    t2m, t2.at[y, :, cols(x)], dev(plane * yy + NX * z + xx, s), 8 + yy, 10 + y
                ).start()

    swap_r.wait_recv()
    for i in range(NX + 1):
        store_win(rm, merged(load_win(rown, i), load_win(rsib, i), s), i)
    to_r = []
    for i in range(NX):
        there = NX * g + 2 + i
        copy = remote(rm.at[pl.ds(i, 2)], rr.at[:, :, cols(x)], dev(there, s), 12 + i, 9)
        go = x != i + 2 if i < 2 else there < n_tm
        to_r.append((go, copy))

        @pl.when(go)
        def _():
            copy.start()

        if i < 2:
            @pl.when(x == i + 2)
            def _():
                for j in range(2):
                    rr[j, :, cols(x)] = rm[i + j]

    @pl.when(p > 0)
    def _():
        ahead.wait_recv()
        for ss in range(2):
            columns_moved(9, 2, 16 * ss)
        inward(2, lambda k, v: store_state(cpi, v, k))

    @pl.when(first_slab)
    def _():
        up[...] = jnp.zeros_like(up)
        for k in range(2):
            store_state(cpi, load_state(init), k)

    v = relax([load_state(cpi, 0), load_state(cpi, 1)], c1, src)
    store_state(relm, v[0])
    store_state(rel, v[1], 0)

    @pl.when(first_slab)
    def _():
        store_state(relm, load_state(init))

    v = relax([load_state(relm), load_state(rel, 0)], c1, src)
    store_state(dfc, sub(v[0], load_state(rel, 0)), 0)
    store_state(prl, v[1], 0)

    def climb(k, v):
        d = sub(load_state(prl, k - 1), load_state(rel, k))
        store_state(dfc, d, k)
        return add(advance([v], c8, -1, 1)[0], d)

    v = lax.fori_loop(1, M, climb, load_state(dfc, 0))

    store_state(mid, v)

    @pl.when(p > 0)
    def _():
        to_up.wait_recv()

    store_state(mid, add(load_state(mid), load_state(up)))
    to_lag = remote(mid, lag, dev(p + 1, s), 6, 6)

    @pl.when(p < n_tm - 1)
    def _():
        to_lag.start()

    @pl.when(p < 2)
    def _():
        rr[...] = jnp.zeros_like(rr)

    @pl.when(first_slab)
    def _():
        lag[...] = jnp.zeros_like(lag)

    q = jnp.maximum(p - 2, 0)
    n = lax.rem(q, plane)
    yq = lax.div(q, plane)
    fbuf[...] = jnp.zeros_like(fbuf)
    for yy in range(n_y - 1):
        @pl.when(yy < yq)
        def _():
            if yy > 0:
                v = move(load_state(fbuf), c64, (plane - 4) // 4, 2, 2)
            whole(t2.at[yy], 10 + yy).wait_recv()
            t2i[...] = permuted(t2[yy], perm_in[...])
            if yy > 0:
                for _ in range(2):
                    (v,) = advance([v], c64, -1, 2)
            f = load_state(t2i)
            store_state(fbuf, add(v, f) if yy > 0 else f)

    n = jnp.where(yq > 0, n, 0)
    f = move(load_state(fbuf), c64, lax.div(n, 4), 2, 2)
    f = move(f, c64, lax.div(lax.rem(n, 4), 2))
    f = move(f, c64, lax.rem(n, 2), 1)

    @pl.when(x >= 2)
    def _():
        whole(rr.at[:, :, pl.ds(0, W - 128)], 9).wait_recv()

    @pl.when(jnp.logical_and(x < 2, g > 0))
    def _():
        whole(rr, 9).wait_recv()

    @pl.when(p > 0)
    def _():
        to_lag.wait_recv()

    rri[...] = permuted(rr[...].reshape(2 * NY, W), perm_in[...]).reshape(2, NY, W)

    e = add(f, load_state(rri, 0))
    (f,) = advance([f], c64, -1, 1)
    last = add(add(f, load_state(rri, 1)), load_state(mid))

    def emit(k, value):
        for c in range(C):
            for r in range(R):
                rows[c, pl.ds(r, 8, stride=R), :] = value[c][r]
        for c in range(C):
            for t in range(2):
                outi[k, pl.ds(8 * t, 8), pl.ds(128 * c, 128)] = rows[c, pl.ds(pl.multiple_of(row0 + 8 * t, 8), 8), :]

    emit(M - 1, add(last, load_state(rel, M - 1)))

    def errors(i, v):
        k = 2 * i
        one, two = two_steps(v, load_state(dfc, k), load_state(dfc, k + 1), c8)
        emit(k, add(one, load_state(rel, k)))
        emit(k + 1, add(two, load_state(rel, k + 1)))
        return two

    v = lax.fori_loop(0, M // 2 - 1, errors, add(load_state(lag), e))
    v = add(advance([v], c8, -1, 1)[0], load_state(dfc, M - 2))
    emit(M - 2, add(v, load_state(rel, M - 2)))
    outb[...] = permuted(outi[...].reshape(M * 16, W), perm_out[...]).reshape(M, 16, W)
    done = pltpu.make_async_copy(outb, out, loc.at[1])
    done.start()

    for yy in range(n_y - 1):
        @pl.when(jnp.logical_and(yy >= yq, yy < y))
        def _():
            whole(t2.at[yy], 10 + yy).wait_recv()

    sib.wait_send()

    @pl.when(p < n_tm - 1)
    def _():
        ahead.wait_send()
        to_up.wait_send()
        to_lag.wait_send()

    for copy in (to_x, shared, to_z, swap_t, swap_r):
        copy.wait_send()
    for yy in range(1, n_y):
        @pl.when(yy > y)
        def _():
            whole(t2.at[0], 8 + yy).wait_send()

    for go, copy in to_r:
        @pl.when(go)
        def _():
            copy.wait_send()

    done.wait()


def body(n_tm, *args):
    def vmem(*shape, dtype=F32):
        return pltpu.VMEM(shape, dtype)

    def state(*lead):
        return vmem(*lead, NY, W)

    def window(*lead):
        return vmem(*lead, NY, 128)

    square = vmem(W, W, dtype=BF16)
    scratch = [
        state(11), square, vmem(W, 2 * W, dtype=BF16), square,
        state(5), vmem(5, NY, W + 256), vmem(5, NY, W + 256), state(), state(),
        window(len(ONE)), window(len(TWO)), window(len(FOUR)), vmem(5 * NY, W),
        vmem(C, 9 * NY, 128), state(4), state(9), state(9), state(), state(M),
        state(), state(), state(), state(), state(), state(), state(),
        vmem(NY, 2 * W), window(2 * NX), window(NZ), window(),
        window(), window(), window(), state(n_tm // (NX * NZ) - 1),
        window(NX + 1), window(NX + 1), window(NX + 1), state(2), state(2), state(),
        state(), vmem(M, 16, W), vmem(M, 16, W),
        pltpu.SemaphoreType.DMA((16,)), pltpu.SemaphoreType.DMA((24,)), pltpu.SemaphoreType.DMA((2,)),
        pltpu.SemaphoreType.REGULAR((3,)),
    ]
    return pl.pallas_call(
        functools.partial(kernel, n_tm),
        out_shape=jax.ShapeDtypeStruct(args[0].shape, F32),
        in_specs=[pl.BlockSpec(memory_space=pltpu.HBM)] * 6,
        out_specs=pl.BlockSpec(memory_space=pltpu.HBM),
        scratch_shapes=scratch,
        compiler_params=pltpu.CompilerParams(
            collective_id=0, has_side_effects=True, vmem_limit_bytes=60 * 1024 * 1024
        ),
    )(*args)


def solution(mesh):
    placed = (
        P("tm", "space", None),
        P("space", None),
        P("space", None),
        P("space", None),
        P("space", None),
        P("space", None),
    )
    return jax.shard_map(
        functools.partial(body, mesh.shape["tm"]),
        mesh=mesh, in_specs=placed, out_specs=P("tm", "space", None), check_vma=False,
    )
```
